128 devices in a mesh: xy: 32 (over x, z, core), gz: 4 (over y).
Axes of the slice: x: 4, y: 4, z: 4, core: 2. Of those that a mesh axis runs over, the one named last changes fastest.
Arguments:
- concentration: float32 [2048, 32, 2048], P('xy', 'gz'), may hold values from -1 to 1
- psi_level: int32 [2048, 32, 2048], P('xy', 'gz'), may hold values from 0 to 4095
- tile_mask: int32 [16, 16], replicated, may hold values 0 or 1
Outputs:
- chem_potential: float32 [2048, 32, 2048], P('xy', 'gz')
- increment: float32 [2048, 32, 2048], P('xy', 'gz')
The draws below stay inside these ranges and needn't reach their ends.
All inputs are finite; a program needn't handle non-finite values.
Results may differ from the reference program's by a relative error of at most 0.0012.
Values sent between devices are 32-bit elements; how exact they have to be, the bound alone decides.
No kernel may reach another device: no remote copies, remote signals or barrier semaphores. Data moves between devices by JAX's collectives and lax.ppermute only.
A program may use at most 128 MiB of HBM per device.

```python
import jax
import jax.numpy as jnp
from jax import lax

NX = 2048
NY = 2048
TILE = 128
LEVELS = 4096
NZ = 32
STIFF = 4096


def set_ends(entries, key, smallest, top_value):
    spot = [jax.random.randint(jax.random.fold_in(key, axis), (), 0, length) for axis, length in enumerate(entries.shape)]
    widest = entries.shape.index(max(entries.shape))
    beside = spot[:widest] + [(spot[widest] + 1) % entries.shape[widest]] + spot[widest + 1:]
    return entries.at[tuple(spot)].set(smallest).at[tuple(beside)].set(top_value)


def shard_levels(stream_key, dims, pieces, smallest, largest):
    def one(dim, parts):
        steps = jax.random.uniform(jax.random.fold_in(jax.random.fold_in(stream_key, 6), dim), (parts,), jnp.float32, smallest / len(pieces), largest / len(pieces))
        return jnp.repeat(jnp.exp(steps), dims[dim] // parts).reshape((-1,) + (1,) * (len(dims) - dim - 1))

    loudness = one(*pieces[0])
    for cut in pieces[1:]:
        loudness = loudness * one(*cut)
    return loudness


def setup_inputs(seed: int = 0) -> dict:
    seeds = jax.random.split(jax.random.key(seed), 4)
    concentration = jnp.clip(jax.random.uniform(seeds[0], (NX, NZ, NY), jnp.float32, -1.0, 1.0) * shard_levels(seeds[0], (NX, NZ, NY), ((0, 32), (1, 4)), -0.4, 0.0), -1.0, 1.0)
    psi_level = set_ends(jax.random.randint(seeds[1], (NX, NZ, NY), 0, LEVELS), jax.random.fold_in(seeds[1], 1), 0, LEVELS - 1).astype(jnp.int32)
    tile_mask = set_ends((jax.random.randint(seeds[2], (NX // TILE, NY // TILE), 0, 2) < 1).astype(jnp.int32), jax.random.fold_in(seeds[2], 1), 0, 1)
    return {"concentration": concentration, "psi_level": psi_level, "tile_mask": tile_mask}


GRADIENT_COEF = 0.5
TIME_STEP = 32.0
PSI_FLOOR = 0.25

def neighbours(padded):
    return [padded[:-2, 1:-1, 1:-1], padded[2:, 1:-1, 1:-1], padded[1:-1, :-2, 1:-1], padded[1:-1, 2:, 1:-1], padded[1:-1, 1:-1, :-2], padded[1:-1, 1:-1, 2:]]

def divergence(values, weights):
    centre_value = values[1:-1, 1:-1, 1:-1]
    centre_psi = weights[1:-1, 1:-1, 1:-1]
    total = jnp.zeros_like(centre_value)
    for near_value, near_psi in zip(neighbours(values), neighbours(weights)):
        both = centre_psi + near_psi
        weight = 2.0 * centre_psi * near_psi / jnp.where(both > 0.0, both, 1.0)
        total = total + weight * (near_value - centre_value)
    return total / jnp.where(centre_psi > 0.0, centre_psi, 1.0)

def implicit_solve(matrix):
    length = matrix.shape[0]
    index = jnp.arange(length)
    ends = (index == 0).astype(matrix.dtype) + (index == length - 1).astype(matrix.dtype)
    diag = 1.0 + STIFF * (2.0 - ends)
    lower = jnp.where(index == 0, 0.0, -STIFF * 1.0).astype(matrix.dtype)
    upper = jnp.where(index == length - 1, 0.0, -STIFF * 1.0).astype(matrix.dtype)
    return lax.linalg.tridiagonal_solve(lower, diag.astype(matrix.dtype), upper, matrix)

def reference(concentration, psi_level, tile_mask):
    psi = PSI_FLOOR + (1.0 - PSI_FLOOR) * psi_level.astype(jnp.float32) / (LEVELS - 1)
    conc_pad = jnp.pad(concentration, 1)
    psi_pad = jnp.pad(psi, 1)
    potential = concentration * concentration * concentration - concentration - GRADIENT_COEF * divergence(conc_pad, psi_pad)
    active = jnp.repeat(jnp.repeat(tile_mask.astype(jnp.float32), TILE, 0), TILE, 1)
    right_side = active[:, None, :] * (TIME_STEP * divergence(jnp.pad(potential, 1), psi_pad))
    lines = implicit_solve(right_side.reshape(NX, NZ * NY)).reshape(NX, NZ, NY)
    turned = jnp.transpose(lines, (2, 0, 1)).reshape(NY, NX * NZ)
    solved = implicit_solve(turned).reshape(NY, NX, NZ)
    increment = jnp.transpose(solved, (1, 2, 0))
    return (potential, increment)
```

```python
import functools
import math

import jax
import jax.numpy as jnp
import numpy as np
from jax import lax
from jax.experimental import pallas as pl
from jax.experimental.pallas import tpu as pltpu
from jax.sharding import PartitionSpec as P

TILE = 128
LEVELS = 4096
STIFF = 4096
GRADIENT_COEF = 0.5
TIME_STEP = 32.0
PSI_FLOOR = 0.25

X = 64
Z = 8
Y = 2048
YT = 16
LANES = 128
ROW = YT * Z
ROWS = X * ROW
FACE = X * YT
LINE = 2048
NB = 256
F32 = jnp.float32
BF16 = jnp.bfloat16

_half = 1.0 + 0.5 / STIFF
THETA = math.log(_half + math.sqrt(_half * _half - 1.0))
RHO = math.exp(-THETA)
GAIN = (RHO / STIFF) / (1.0 - RHO * RHO)


def rho(power):
    return math.exp(-THETA * power)


def vmem(limit_mib):
    return pltpu.CompilerParams(vmem_limit_bytes=limit_mib * 2**20)


def half_over_psi(level):
    return 0.5 / (PSI_FLOOR + level.astype(F32) * ((1.0 - PSI_FLOOR) / (LEVELS - 1)))


def recip(value):
    return 1.0 / value


def lane_iota(shape):
    return lax.broadcasted_iota(jnp.int32, shape, len(shape) - 1)


def sub_iota(shape):
    return lax.broadcasted_iota(jnp.int32, shape, len(shape) - 2)


def next_y(v):
    axis = v.ndim - 1
    turned = pltpu.roll(v, LANES - 1, axis)
    if TILES_LEAD[v.shape[-2]]:
        following = jnp.concatenate([turned[1:], turned[:1]], axis=0)
    else:
        following = pltpu.roll(turned, YT - 1, axis - 1)
    return jnp.where(lane_iota(v.shape) == LANES - 1, following, turned)


def prev_y(v):
    axis = v.ndim - 1
    turned = pltpu.roll(v, 1, axis)
    if TILES_LEAD[v.shape[-2]]:
        previous = jnp.concatenate([turned[-1:], turned[:-1]], axis=0)
    else:
        previous = pltpu.roll(turned, 1, axis - 1)
    return jnp.where(lane_iota(v.shape) == 0, previous, turned)


TILES_LEAD = {Z: True, YT: False}


def next_z(v):
    return pltpu.roll(v, Z - 1, 1)


def prev_z(v):
    return pltpu.roll(v, 1, 1)


PRE_X = 16


def faces_kernel(c_ref, l_ref, zlo_ref, zhi_ref, in_ref, xlo_ref, xhi_ref):
    step = pl.program_id(0)

    def plane(ref, z):
        return ref[pl.ds(z, PRE_X * YT, stride=Z), :]

    for out, edge, inner, spot in ((zlo_ref, 0, 1, 0), (zhi_ref, 7, 6, 1)):
        c_edge, c_inner = plane(c_ref, edge), plane(c_ref, inner)
        h_edge = half_over_psi(plane(l_ref, edge))
        h_inner = half_over_psi(plane(l_ref, inner))
        out[0] = c_edge
        out[1] = h_edge
        out[2] = recip(h_edge + h_inner) * (c_inner - c_edge)
        in_ref[spot] = h_inner

    @pl.when(step == 0)
    def _():
        xlo_ref[0] = c_ref[0:2 * ROW, :]
        xlo_ref[1] = half_over_psi(l_ref[0:2 * ROW, :])

    @pl.when(step == X // PRE_X - 1)
    def _():
        last = (PRE_X - 2) * ROW
        xhi_ref[0] = c_ref[last:last + 2 * ROW, :]
        xhi_ref[1] = half_over_psi(l_ref[last:last + 2 * ROW, :])


def make_faces(c, level):
    block = pl.BlockSpec((PRE_X * ROW, LANES), lambda i: (i, 0))
    face = pl.BlockSpec((3, PRE_X * YT, LANES), lambda i: (0, i, 0))
    inner = pl.BlockSpec((2, PRE_X * YT, LANES), lambda i: (0, i, 0))
    whole = pl.BlockSpec((2, 2 * ROW, LANES), lambda i: (0, 0, 0))
    return pl.pallas_call(
        faces_kernel,
        grid=(X // PRE_X,),
        in_specs=[block, block],
        out_specs=[face, face, inner, whole, whole],
        out_shape=[
            jax.ShapeDtypeStruct((3, FACE, LANES), F32),
            jax.ShapeDtypeStruct((3, FACE, LANES), F32),
            jax.ShapeDtypeStruct((2, FACE, LANES), F32),
            jax.ShapeDtypeStruct((2, 2 * ROW, LANES), F32),
            jax.ShapeDtypeStruct((2, 2 * ROW, LANES), F32),
        ],
        compiler_params=vmem(40),
        cost_estimate=pl.CostEstimate(flops=10**6, bytes_accessed=13 * 2**20, transcendentals=0),
        name="faces",
    )(c, level)


def y_tables():
    idx = np.arange(NB)
    table = GAIN * np.exp(-THETA * np.abs(idx[:, None] - idx[None, :]))
    high = table.astype(jnp.bfloat16)
    low = (table - high.astype(np.float64)).astype(jnp.bfloat16)
    fwd = np.exp(-THETA * (idx + 1.0))
    bwd = np.exp(-THETA * (NB - idx.astype(np.float64)))
    edge = np.zeros((8, LANES), np.float32)
    edge[0], edge[1] = fwd[:LANES], fwd[LANES:]
    edge[2], edge[3] = bwd[:LANES], bwd[LANES:]
    return high, low, edge


def split(v):
    high = v.astype(BF16)
    return high, (v - high.astype(F32)).astype(BF16)


def dot3(a, b):
    (a_high, a_low), (b_high, b_low) = a, b
    mm = functools.partial(jnp.dot, preferred_element_type=F32)
    return mm(a_high, b_high) + (mm(a_low, b_high) + mm(a_high, b_low))


def ends(first, last, length):
    scale = 1.0 / (1.0 - rho(2 * length))
    tail = rho(length)
    return (first + tail * last) * scale, (last + tail * first) * scale


def y_carry(tiles, edge):
    count = YT // 2
    heads = [tiles[2 * b][:, 0:1] for b in range(count)]
    tails = [tiles[2 * b + 1][:, LANES - 1:LANES] for b in range(count)]
    hop = rho(NB)
    right = [jnp.zeros_like(heads[0])]
    for b in range(count - 1):
        right.append(hop * right[-1] + tails[b])
    left = [jnp.zeros_like(heads[0])]
    for b in range(count - 1, 0, -1):
        left.append(hop * left[-1] + heads[b])
    left = left[::-1]
    from_low, from_high = ends(heads[0] + hop * left[0], tails[-1] + hop * right[-1], Y)
    out = []
    for b in range(count):
        carry_r = right[b] + rho(NB * b) * from_low
        carry_l = left[b] + rho(NB * (count - 1 - b)) * from_high
        for k in range(2):
            out.append(tiles[2 * b + k] + carry_r * edge[k:k + 1, :] + carry_l * edge[2 + k:3 + k, :])
    return out


CHUNK = 8
NCHUNK = X // CHUNK
MROWS = 16


def block_kernel(flag_ref, c_hbm, l_hbm, xlo_ref, xhi_ref, act_ref, thigh_ref, tlow_ref, edge_ref,
                 pot_hbm, v_hbm, mom_ref, edgepot_ref,
                 c_s, l_s, pot_s, f_s, u_s, st, in_sem, pot_sem, v_sem):
    def copies_in(i):
        at = pl.ds(i * CHUNK, CHUNK)
        return (pltpu.make_async_copy(c_hbm.at[at], c_s.at[at], in_sem.at[0, i]),
                pltpu.make_async_copy(l_hbm.at[at], l_s.at[at], in_sem.at[1, i]))

    for i in range(NCHUNK):
        for copy in copies_in(i):
            copy.start()

    shape = (YT, Z, LANES)
    open_z = lax.broadcasted_iota(jnp.int32, shape, 1) < Z - 1
    open_y = jnp.logical_or(
        lax.broadcasted_iota(jnp.int32, shape, 2) < LANES - 1,
        lax.broadcasted_iota(jnp.int32, shape, 0) < YT - 1,
    )
    C1, H1, A1, FX2, WZ1, WY1, WX2, POT2, H2, B2, GX3, PF = range(12)

    def advance(c, h, open_x, emit):
        h1, c1 = st[H1], st[C1]
        wx1 = recip(h1 + h) * open_x
        fx1 = wx1 * (c - c1)
        wz = jnp.where(open_z, recip(h + next_z(h)), 0.0)
        wy = jnp.where(open_y, recip(h + next_y(h)), 0.0)
        fz = wz * (next_z(c) - c)
        fy = wy * (next_y(c) - c)
        across = (fz - prev_z(fz)) + (fy - prev_y(fy))
        pot1 = c1 * (c1 * c1 - 1.0) - h1 * (st[A1] + fx1 - st[FX2])
        gx2 = st[WX2] * (pot1 - st[POT2])
        gz = st[WZ1] * (next_z(pot1) - pot1)
        gy = st[WY1] * (next_y(pot1) - pot1)
        across2 = (gz - prev_z(gz)) + (gy - prev_y(gy))
        if emit is not None:
            rhs = act_ref[...] * (st[H2] * (st[B2] + gx2 - st[GX3]))
            forward = RHO * st[PF] + rhs
            st[PF] = forward
            f_s[emit] = rhs
            u_s[emit] = forward
            pot_s[prow(emit), :] = st[POT2].reshape(ROW, LANES)
        st[A1] = across
        st[FX2] = fx1
        st[WZ1] = wz
        st[WY1] = wy
        st[WX2] = wx1
        st[POT2] = pot1
        st[H2] = h1
        st[B2] = across2
        st[GX3] = gx2
        st[C1] = c
        st[H1] = h

    def prow(x):
        return pl.ds(pl.multiple_of(x * ROW, ROW), ROW)

    for k in range(12):
        st[k] = jnp.zeros(shape, F32)
    open_lo, open_hi = flag_ref[0], flag_ref[1]
    ones = jnp.ones(shape, F32)
    st[H1] = ones
    advance(xlo_ref[0, 0], jnp.where(open_lo > 0.0, xlo_ref[1, 0], ones), 0.0, None)
    advance(xlo_ref[0, 1], jnp.where(open_lo > 0.0, xlo_ref[1, 1], ones), open_lo, None)

    def main(x, emit):
        advance(c_s[x], half_over_psi(l_s[x]), jnp.where(x == 0, open_lo, 1.0), emit)

    for copy in copies_in(0):
        copy.wait()
    main(0, None)
    main(1, None)

    def rows_loop(first, last):
        def body(x, _):
            main(x, x - 2)
            return 0
        lax.fori_loop(first, last, body, 0)

    def pot_copy(i):
        at = pl.ds(i * CHUNK * ROW, CHUNK * ROW)
        return pltpu.make_async_copy(pot_s.at[at], pot_hbm.at[at], pot_sem.at[i])

    rows_loop(2, CHUNK)
    for i in range(1, NCHUNK):
        for copy in copies_in(i):
            copy.wait()
        rows_loop(i * CHUNK, (i + 1) * CHUNK)
        pot_copy(i - 1).start()
    advance(xhi_ref[0, 0], jnp.where(open_hi > 0.0, xhi_ref[1, 0], ones), open_hi, X - 2)
    advance(xhi_ref[0, 1], jnp.where(open_hi > 0.0, xhi_ref[1, 1], ones), open_hi, X - 1)
    pot_copy(NCHUNK - 1).start()

    def back(k, carry):
        x = X - 1 - k
        f = f_s[x]
        u_s[x] = GAIN * (u_s[x] + carry)
        return RHO * (carry + f)

    lax.fori_loop(0, X, back, jnp.zeros(shape, F32))
    mom_ref[0] = u_s[X - 1]
    mom_ref[1] = u_s[0]
    for side, z in ((0, 0), (1, 7)):
        edgepot_ref[side] = pot_s[pl.ds(z, FACE, stride=Z), :]

    def blocks(i, _):
        xs = pl.ds(i * MROWS, MROWS)
        table = (thigh_ref[...], tlow_ref[...])
        for b in range(YT // 2):
            pair = [u_s[xs, 2 * b + k].reshape(MROWS * Z, LANES) for k in range(2)]
            solved = dot3(split(jnp.concatenate(pair, axis=1)), table)
            for k in range(2):
                f_s[xs, 2 * b + k] = solved[:, k * LANES:(k + 1) * LANES].reshape(MROWS, Z, LANES)
        return 0

    lax.fori_loop(0, X // MROWS, blocks, 0)
    edge = edge_ref[...]

    def v_copy(i):
        at = pl.ds(i * CHUNK, CHUNK)
        return pltpu.make_async_copy(u_s.at[at], v_hbm.at[at], v_sem.at[i])

    for i in range(NCHUNK):
        def body(x, _):
            for t, part in enumerate(y_carry([f_s[x, t] for t in range(YT)], edge)):
                u_s[x, t] = part
            return 0
        lax.fori_loop(i * CHUNK, (i + 1) * CHUNK, body, 0)
        v_copy(i).start()
    for i in range(NCHUNK):
        pot_copy(i).wait()
        v_copy(i).wait()


def solve_block(flags, c, level, xlo, xhi, act, tables):
    any_spec = pl.BlockSpec(memory_space=pl.ANY)
    vm = pl.BlockSpec(memory_space=pltpu.VMEM)
    block = (X, YT, Z, LANES)
    return pl.pallas_call(
        block_kernel,
        in_specs=[pl.BlockSpec(memory_space=pltpu.SMEM), any_spec, any_spec] + [vm] * 6,
        out_specs=[any_spec, any_spec, vm, vm],
        out_shape=[
            jax.ShapeDtypeStruct((ROWS, LANES), F32),
            jax.ShapeDtypeStruct(block, F32),
            jax.ShapeDtypeStruct((2, YT, Z, LANES), F32),
            jax.ShapeDtypeStruct((2, FACE, LANES), F32),
        ],
        scratch_shapes=[
            pltpu.VMEM(block, F32),
            pltpu.VMEM(block, jnp.int32),
            pltpu.VMEM((ROWS, LANES), F32),
            pltpu.VMEM(block, F32),
            pltpu.VMEM(block, F32),
            pltpu.VMEM((12, YT, Z, LANES), F32),
            pltpu.SemaphoreType.DMA((2, NCHUNK)),
            pltpu.SemaphoreType.DMA((NCHUNK,)),
            pltpu.SemaphoreType.DMA((NCHUNK,)),
        ],
        compiler_params=vmem(44),
        cost_estimate=pl.CostEstimate(flops=4 * 10**9, bytes_accessed=60 * 2**20, transcendentals=0),
        name="block",
    )(flags, c.reshape(block), level.reshape(block), xlo, xhi, act, *tables)


EXT = X + 2
GROUP = 8


def seam_kernel(flag_ref, pow_ref, own_lo_ref, own_hi_ref, inner_ref, got_lo_ref, got_hi_ref, xlo_ref, xhi_ref,
                corner_lo_ref, corner_hi_ref, edgepot_ref, mom_ref, act_ref,
                df_ref, dpot_ref, send_ref, c0_s, h0_s, cm_s, hm_s, fl_s, dp_s, acc_s):
    open_x = (flag_ref[0], flag_ref[1])
    act = act_ref[:, 0, :]
    shape = (GROUP, YT, LANES)
    open_y = jnp.logical_or(
        lax.broadcasted_iota(jnp.int32, shape, 2) < LANES - 1,
        lax.broadcasted_iota(jnp.int32, shape, 1) < YT - 1,
    )
    row = lax.broadcasted_iota(jnp.int32, shape, 0)
    acc_s[...] = jnp.zeros_like(acc_s)

    for side, (own, got, corner, z) in enumerate(
        ((own_lo_ref, got_lo_ref, corner_lo_ref, 0), (own_hi_ref, got_hi_ref, corner_hi_ref, 7))
    ):
        open_z = flag_ref[2 + side]
        main = slice(1, 1 + X)
        c0_s[main] = own[0]
        h0_s[main] = own[1]
        cm_s[main] = got[0]
        hm_s[main] = jnp.where(open_z > 0.0, got[1], 1.0)
        for spot, ref, r, k in ((0, xlo_ref, 1, 0), (EXT - 1, xhi_ref, 0, 1)):
            inside = open_x[k] > 0.0
            both = open_x[k] * open_z > 0.0
            c0_s[spot] = ref[0, r, :, z, :]
            h0_s[spot] = jnp.where(inside, ref[1, r, :, z, :], 1.0)
            cm_s[spot] = corner[2 * k]
            hm_s[spot] = jnp.where(both, corner[2 * k + 1], 1.0)

        def first(i, _):
            at = pl.ds(i * 6, 6)
            h0 = h0_s[at]
            flux = recip(h0 + hm_s[at]) * open_z * (cm_s[at] - c0_s[at])
            fl_s[at] = flux
            dp_s[at] = -h0 * flux
            return 0

        lax.fori_loop(0, EXT // 6, first, 0)

        def second(i, _):
            at = pl.ds(i * GROUP, GROUP)
            ext = pl.ds(i * GROUP + 1, GROUP)
            after = pl.ds(i * GROUP + 2, GROUP)
            lo_gate = jnp.where(row == 0, jnp.where(i == 0, open_x[0], 1.0), 1.0)
            hi_gate = jnp.where(row == GROUP - 1, jnp.where(i == X // GROUP - 1, open_x[1], 1.0), 1.0)

            def plane(h_ref, v_ref):
                h, v = h_ref[ext], v_ref[ext]
                wy = jnp.where(open_y, recip(h + next_y(h)), 0.0)
                fy = wy * (next_y(v) - v)
                total = recip(h + h_ref[at]) * lo_gate * (v_ref[at] - v)
                total = total + recip(h + h_ref[after]) * hi_gate * (v_ref[after] - v)
                return h, v, total + (fy - prev_y(fy))

            hm, cm, across_m = plane(hm_s, cm_s)
            h0, dp, across_0 = plane(h0_s, dp_s)
            flux = fl_s[ext]
            potm = cm * (cm * cm - 1.0) - hm * (across_m + got[2, at] - flux)
            pot0 = edgepot_ref[side, at] + dp
            h1 = inner_ref[side, at]
            toward = recip(h0 + h1) * dp
            join = recip(h0 + hm) * open_z * (potm - pot0)
            df0 = act * (h0 * (across_0 - toward + join))
            df1 = act * (h1 * toward)
            outer, inner = (0, 1) if side == 0 else (3, 2)
            df_ref[outer, at] = df0
            df_ref[inner, at] = df1
            dpot_ref[side, at] = dp
            for spot, value in ((outer, df0), (inner, df1)):
                last, start = acc_s[spot], acc_s[4 + spot]
                for r in range(GROUP):
                    x = i * GROUP + r
                    last = last + pow_ref[1, X - 1 - x] * value[r]
                    start = start + pow_ref[1, x] * value[r]
                acc_s[spot] = last
                acc_s[4 + spot] = start
            return 0

        lax.fori_loop(0, X // GROUP, second, 0)

    sub = sub_iota((Z, LANES))
    half = sub < 4
    for t in range(YT):
        totals = []
        for which in range(2):
            total = mom_ref[which, t]
            for k, z in enumerate((0, 1, 6, 7)):
                line = jnp.broadcast_to(acc_s[4 * which + k, t:t + 1, :], (Z, LANES))
                total = total + jnp.where(sub == z, line, 0.0)
            totals.append(total)
        last, start = totals
        send_ref[2 * t] = jnp.where(half, last, pltpu.roll(start, 4, 0))
        send_ref[2 * t + 1] = jnp.where(half, pltpu.roll(last, 4, 0), start)


def add_seams(flags, powers, own_lo, own_hi, inner, got_lo, got_hi, xlo, xhi, corner_lo, corner_hi, edgepot, mom, act):
    vm = pl.BlockSpec(memory_space=pltpu.VMEM)
    sm = pl.BlockSpec(memory_space=pltpu.SMEM)
    lines = [a.reshape(a.shape[0], X, YT, LANES) for a in (own_lo, own_hi, inner, got_lo, got_hi)]
    return pl.pallas_call(
        seam_kernel,
        in_specs=[sm, sm] + [vm] * 12,
        out_specs=[vm, vm, vm],
        out_shape=[
            jax.ShapeDtypeStruct((4, X, YT, LANES), F32),
            jax.ShapeDtypeStruct((2, X, YT, LANES), F32),
            jax.ShapeDtypeStruct((32, Z, LANES), F32),
        ],
        scratch_shapes=[pltpu.VMEM((EXT, YT, LANES), F32)] * 6 + [pltpu.VMEM((8, YT, LANES), F32)],
        compiler_params=vmem(40),
        cost_estimate=pl.CostEstimate(flops=10**7, bytes_accessed=12 * 2**20, transcendentals=0),
        name="seams",
    )(flags, powers, *lines, xlo, xhi, corner_lo, corner_hi, edgepot.reshape(2, X, YT, LANES), mom, act)


def planes_kernel(df_ref, thigh_ref, tlow_ref, edge_ref, out_ref, p_s, u_s, w_s):
    shape = (4, YT, LANES)

    def forth(x, carry):
        carry = RHO * carry + df_ref[:, x]
        p_s[:, x] = carry
        return carry

    lax.fori_loop(0, X, forth, jnp.zeros(shape, F32), unroll=4)

    def back(k, carry):
        x = X - 1 - k
        solved = GAIN * (p_s[:, x] + carry)
        at = pl.ds(pl.multiple_of(x * YT, YT), YT)
        for z in range(4):
            u_s[z, at, :] = solved[z]
        return RHO * (carry + df_ref[:, x])

    lax.fori_loop(0, X, back, jnp.zeros(shape, F32), unroll=4)

    table = (thigh_ref[...], tlow_ref[...])
    edge = edge_ref[...]
    for z in range(4):
        for b in range(YT // 2):
            pair = [u_s[z, pl.ds(2 * b + k, X, stride=YT), :] for k in range(2)]
            solved = dot3(split(jnp.concatenate(pair, axis=1)), table)
            for k in range(2):
                w_s[z, 2 * b + k] = solved[:, k * LANES:(k + 1) * LANES]

    for z in range(4):
        def body(i, _):
            at = pl.ds(pl.multiple_of(i * 8, 8), 8)
            parts = y_carry([w_s[z, t, at, :] for t in range(YT)], edge)
            for t, part in enumerate(parts):
                out_ref[z, pl.ds(i * 8 * YT + t, 8, stride=YT), :] = part
            return 0
        lax.fori_loop(0, X // 8, body, 0)


def solve_planes(df, tables):
    vm = pl.BlockSpec(memory_space=pltpu.VMEM)
    return pl.pallas_call(
        planes_kernel,
        in_specs=[vm] * 4,
        out_specs=vm,
        out_shape=jax.ShapeDtypeStruct((4, FACE, LANES), F32),
        scratch_shapes=[
            pltpu.VMEM((4, X, YT, LANES), F32),
            pltpu.VMEM((4, FACE, LANES), F32),
            pltpu.VMEM((4, YT, X, LANES), F32),
        ],
        compiler_params=vmem(40),
        cost_estimate=pl.CostEstimate(flops=2 * 10**9, bytes_accessed=10 * 2**20, transcendentals=0),
        name="planes",
    )(df, *tables)


def mend_kernel(pot_ref, dpot_ref, out_ref):
    out_ref[...] = pot_ref[...]
    for side, z in ((0, 0), (1, 7)):
        at = pl.ds(z, PRE_X * YT, stride=Z)
        out_ref[at, :] = pot_ref[at, :] + dpot_ref[side]


def mend_potential(pot, dpot):
    block = pl.BlockSpec((PRE_X * ROW, LANES), lambda i: (i, 0))
    return pl.pallas_call(
        mend_kernel,
        grid=(X // PRE_X,),
        in_specs=[block, pl.BlockSpec((2, PRE_X * YT, LANES), lambda i: (0, i, 0))],
        out_specs=block,
        out_shape=jax.ShapeDtypeStruct((ROWS, LANES), F32),
        compiler_params=vmem(40),
        cost_estimate=pl.CostEstimate(flops=10**6, bytes_accessed=9 * 2**20, transcendentals=0),
        name="mend",
    )(pot, dpot.reshape(2, FACE, LANES))


def carries_kernel(count, in_ref, out_ref):
    got = [in_ref[d] for d in range(count)]
    half = sub_iota((8, TILE)) < 4
    hop = rho(X)
    right = [jnp.zeros((8, TILE), F32)]
    for d in range(count - 1):
        right.append(hop * right[-1] + got[d])
    starts = [pltpu.roll(g, 4, 0) for g in got]
    left = [jnp.zeros((8, TILE), F32)]
    for d in range(count - 1, 0, -1):
        left.append(hop * left[-1] + starts[d])
    left = left[::-1]
    from_low, from_high = ends(starts[0] + hop * left[0], got[-1] + hop * right[-1], X * count)
    for d in range(count):
        carry_r = right[d] + rho(X * d) * from_low
        carry_l = left[d] + rho(X * (count - 1 - d)) * from_high
        out_ref[d] = jnp.where(half, carry_r, pltpu.roll(carry_l, 4, 0))


def scan_carries(got):
    vm = pl.BlockSpec(memory_space=pltpu.VMEM)
    return pl.pallas_call(
        functools.partial(carries_kernel, got.shape[0]),
        in_specs=[vm],
        out_specs=vm,
        out_shape=jax.ShapeDtypeStruct(got.shape, F32),
        cost_estimate=pl.CostEstimate(flops=10**6, bytes_accessed=2**18, transcendentals=0),
        name="carries",
    )(got)


FIN = 8


def final_kernel(pow_ref, got_ref, thigh_ref, tlow_ref, edge_ref, v_ref, dv_ref, out_ref, lr_s):
    step = pl.program_id(0)

    @pl.when(step == 0)
    def _():
        half = sub_iota((Z, LANES)) < 4
        edge = edge_ref[...]
        raw = []
        for t in range(YT):
            even, odd = got_ref[2 * t], got_ref[2 * t + 1]
            raw.append(jnp.concatenate([
                jnp.where(half, even, pltpu.roll(odd, 4, 0)),
                jnp.where(half, pltpu.roll(even, 4, 0), odd),
            ], axis=0))
        local = []
        for b in range(YT // 2):
            solved = dot3(split(jnp.concatenate(raw[2 * b:2 * b + 2], axis=1)), (thigh_ref[...], tlow_ref[...]))
            local += [solved[:, :LANES], solved[:, LANES:]]
        for side in range(2):
            tiles = [part[8 * side:8 * side + 8, :] for part in local]
            for t, part in enumerate(y_carry(tiles, edge)):
                lr_s[side, t * Z:(t + 1) * Z, :] = part

    for r in range(FIN):
        at = slice(r * ROW, (r + 1) * ROW)
        x = step * FIN + r
        out_ref[at, :] = v_ref[at, :] + pow_ref[0, x] * lr_s[0] + pow_ref[0, X - 1 - x] * lr_s[1]
    for k, z in enumerate((0, 1, 6, 7)):
        at = pl.ds(z, FIN * YT, stride=Z)
        out_ref[at, :] = out_ref[at, :] + dv_ref[k]


def finish(powers, got, tables, v, dv):
    def whole(a):
        return pl.BlockSpec(a.shape, lambda i: (0,) * a.ndim)

    block = pl.BlockSpec((FIN * ROW, LANES), lambda i: (i, 0))
    return pl.pallas_call(
        final_kernel,
        grid=(X // FIN,),
        in_specs=[pl.BlockSpec(memory_space=pltpu.SMEM), whole(got)] + [whole(t) for t in tables]
        + [block, pl.BlockSpec((4, FIN * YT, LANES), lambda i: (0, i, 0))],
        out_specs=block,
        out_shape=jax.ShapeDtypeStruct((ROWS, LANES), F32),
        scratch_shapes=[pltpu.VMEM((2, ROW, LANES), F32)],
        compiler_params=vmem(40),
        cost_estimate=pl.CostEstimate(flops=10**7, bytes_accessed=10 * 2**20, transcendentals=0),
        name="finish",
    )(powers, got, *tables, v, dv)


def shift(value, axis, forward):
    count = lax.axis_size(axis)
    pairs = [(i, i + 1) for i in range(count - 1)]
    if not forward:
        pairs = [(b, a) for a, b in pairs]
    return lax.ppermute(value, axis, pairs)


def to_tiles(block):
    return block.reshape(X, Z, YT, LANES).transpose(0, 2, 1, 3).reshape(ROWS, LANES)


def from_tiles(rows):
    return rows.reshape(X, YT, Z, LANES).transpose(0, 2, 1, 3).reshape(X, Z, Y)


def per_device(concentration, psi_level, tile_mask):
    c, level = to_tiles(concentration), to_tiles(psi_level)
    xy, gz = lax.axis_index("xy"), lax.axis_index("gz")
    n_xy, n_gz = lax.axis_size("xy"), lax.axis_size("gz")
    flags = jnp.stack([xy > 0, xy < n_xy - 1, gz > 0, gz < n_gz - 1]).astype(F32)
    mask_row = lax.dynamic_index_in_dim(tile_mask, xy * X // TILE, 0, keepdims=False)
    act = jnp.broadcast_to((mask_row.astype(F32) * (2.0 * TIME_STEP))[:, None, None], (YT, Z, LANES))
    tables = tuple(jnp.asarray(t) for t in y_tables())
    steps = np.exp(-THETA * np.arange(X + 1))
    powers = jnp.asarray(np.stack([steps[1:], GAIN * steps[:-1]]).astype(np.float32))

    zlo, zhi, inner, xlo, xhi = make_faces(c, level)
    pair = (2, 2, YT, Z, LANES)
    got_xlo = shift(xhi, "xy", True).reshape(pair)
    got_xhi = shift(xlo, "xy", False).reshape(pair)
    got_zlo = shift(zhi, "gz", True)
    got_zhi = shift(zlo, "gz", False)

    def corners(z):
        return jnp.stack([got_xlo[0, 1, :, z], got_xlo[1, 1, :, z], got_xhi[0, 0, :, z], got_xhi[1, 0, :, z]])

    corner_lo = shift(corners(7), "gz", True)
    corner_hi = shift(corners(0), "gz", False)

    pot, v, mom, edgepot = solve_block(flags, c, level, got_xlo, got_xhi, act, tables)
    df, dpot, send = add_seams(
        flags, powers, zlo, zhi, inner, got_zlo, got_zhi, got_xlo, got_xhi, corner_lo, corner_hi, edgepot, mom, act,
    )
    got = lax.all_to_all(send, "xy", split_axis=0, concat_axis=0, tiled=True)
    dv = solve_planes(df, tables)
    potential = mend_potential(pot, dpot)
    back = lax.all_to_all(scan_carries(got), "xy", split_axis=0, concat_axis=0, tiled=True)
    increment = finish(powers, back, tables, v.reshape(ROWS, LANES), dv)
    return from_tiles(potential), from_tiles(increment)


def solution(mesh):
    placed = (P("xy", "gz", None), P("xy", "gz", None), P())
    return jax.shard_map(
        per_device,
        mesh=mesh,
        in_specs=placed,
        out_specs=(P("xy", "gz", None), P("xy", "gz", None)),
        check_vma=False,
    )
```

```python
import functools
import math

import jax
import jax.numpy as jnp
import numpy as np
from jax import lax
from jax.experimental import pallas as pl
from jax.experimental.pallas import tpu as pltpu
from jax.sharding import PartitionSpec as P

TILE = 128
LEVELS = 4096
STIFF = 4096
GRADIENT_COEF = 0.5
TIME_STEP = 32.0
PSI_FLOOR = 0.25

X = 64
Z = 8
Y = 2048
YT = 16
LANES = 128
ROW = YT * Z
ROWS = X * ROW
FACE = X * YT
LINE = 2048
NB = 256
F32 = jnp.float32
BF16 = jnp.bfloat16

_half = 1.0 + 0.5 / STIFF
THETA = math.log(_half + math.sqrt(_half * _half - 1.0))
RHO = math.exp(-THETA)
GAIN = (RHO / STIFF) / (1.0 - RHO * RHO)


def rho(power):
    return math.exp(-THETA * power)


def vmem(limit_mib):
    return pltpu.CompilerParams(vmem_limit_bytes=limit_mib * 2**20)


def half_over_psi(level):
    return recip(2.0 * PSI_FLOOR + level.astype(F32) * (2.0 * (1.0 - PSI_FLOOR) / (LEVELS - 1)))


def recip(value):
    return pl.reciprocal(value, approx=True)


def lane_iota(shape):
    return lax.broadcasted_iota(jnp.int32, shape, len(shape) - 1)


def sub_iota(shape):
    return lax.broadcasted_iota(jnp.int32, shape, len(shape) - 2)


def next_y(v):
    axis = v.ndim - 1
    turned = pltpu.roll(v, LANES - 1, axis)
    if TILES_LEAD[v.shape[-2]]:
        following = jnp.concatenate([turned[1:], turned[:1]], axis=0)
    else:
        following = pltpu.roll(turned, YT - 1, axis - 1)
    return jnp.where(lane_iota(v.shape) == LANES - 1, following, turned)


def prev_y(v):
    axis = v.ndim - 1
    turned = pltpu.roll(v, 1, axis)
    if TILES_LEAD[v.shape[-2]]:
        previous = jnp.concatenate([turned[-1:], turned[:-1]], axis=0)
    else:
        previous = pltpu.roll(turned, 1, axis - 1)
    return jnp.where(lane_iota(v.shape) == 0, previous, turned)


TILES_LEAD = {Z: True, YT: False}


def next_z(v):
    return pltpu.roll(v, Z - 1, 1)


def prev_z(v):
    return pltpu.roll(v, 1, 1)


CHUNK = 8
NCHUNK = X // CHUNK
PART = CHUNK * YT


def faces_kernel(c_hbm, l_hbm, zlo_hbm, zhi_hbm, in_hbm, xlo_ref, xhi_ref, c_s, l_s, z_s, i_s, in_sem, out_sem):
    def arrivals(i):
        at = pl.ds(i * CHUNK * ROW, CHUNK * ROW)
        return (pltpu.make_async_copy(c_hbm.at[at], c_s.at[at], in_sem.at[0, i]),
                pltpu.make_async_copy(l_hbm.at[at], l_s.at[at], in_sem.at[1, i]))

    def departures(i):
        at = pl.ds(i * PART, PART)
        pairs = ((z_s.at[0, :, at], zlo_hbm.at[:, at]), (z_s.at[1, :, at], zhi_hbm.at[:, at]),
                 (i_s.at[:, at], in_hbm.at[:, at]))
        return [pltpu.make_async_copy(near, far, out_sem.at[k, i]) for k, (near, far) in enumerate(pairs)]

    for i in range(NCHUNK):
        for copy in arrivals(i):
            copy.start()

    def chunk(i, _):
        for copy in arrivals(i):
            copy.wait()
        out = pl.ds(i * PART, PART)

        def plane(ref, z):
            return ref[pl.ds(i * CHUNK * ROW + z, PART, stride=Z), :]

        for side, edge, inner in ((0, 0, 1), (1, 7, 6)):
            c_edge, c_inner = plane(c_s, edge), plane(c_s, inner)
            h_edge = half_over_psi(plane(l_s, edge))
            h_inner = half_over_psi(plane(l_s, inner))
            z_s[side, 0, out] = c_edge
            z_s[side, 1, out] = h_edge
            z_s[side, 2, out] = recip(h_edge + h_inner) * (c_inner - c_edge)
            i_s[side, out] = h_inner
        for copy in departures(i):
            copy.start()
        return 0

    lax.fori_loop(0, NCHUNK, chunk, 0)
    last = (X - 2) * ROW
    for ref, at in ((xlo_ref, 0), (xhi_ref, last)):
        ref[0] = c_s[at:at + 2 * ROW, :]
        ref[1] = l_s[at:at + 2 * ROW, :].astype(F32)
    for i in range(NCHUNK):
        for copy in departures(i):
            copy.wait()


def make_faces(c, level):
    hbm = pl.BlockSpec(memory_space=pltpu.HBM)
    vm = pl.BlockSpec(memory_space=pltpu.VMEM)
    return pl.pallas_call(
        faces_kernel,
        in_specs=[hbm, hbm],
        out_specs=[hbm, hbm, hbm, vm, vm],
        out_shape=[
            jax.ShapeDtypeStruct((3, FACE, LANES), F32),
            jax.ShapeDtypeStruct((3, FACE, LANES), F32),
            jax.ShapeDtypeStruct((2, FACE, LANES), F32),
            jax.ShapeDtypeStruct((2, 2 * ROW, LANES), F32),
            jax.ShapeDtypeStruct((2, 2 * ROW, LANES), F32),
        ],
        scratch_shapes=[
            pltpu.VMEM((ROWS, LANES), F32),
            pltpu.VMEM((ROWS, LANES), jnp.int32),
            pltpu.VMEM((2, 3, FACE, LANES), F32),
            pltpu.VMEM((2, FACE, LANES), F32),
            pltpu.SemaphoreType.DMA((2, NCHUNK)),
            pltpu.SemaphoreType.DMA((3, NCHUNK)),
        ],
        compiler_params=vmem(60),
        cost_estimate=pl.CostEstimate(flops=10**6, bytes_accessed=13 * 2**20, transcendentals=0),
        name="faces",
    )(c, level)


def y_tables():
    idx = np.arange(NB)
    table = GAIN * np.exp(-THETA * np.abs(idx[:, None] - idx[None, :]))
    high = table.astype(jnp.bfloat16)
    low = (table - high.astype(np.float64)).astype(jnp.bfloat16)
    fwd = np.exp(-THETA * (idx + 1.0))
    bwd = np.exp(-THETA * (NB - idx.astype(np.float64)))
    edge = np.zeros((8, LANES), np.float32)
    edge[0], edge[1] = fwd[:LANES], fwd[LANES:]
    edge[2], edge[3] = bwd[:LANES], bwd[LANES:]
    return high, low, edge


def split(v):
    high = v.astype(BF16)
    return high, (v - high.astype(F32)).astype(BF16)


def dot3(a, b):
    (a_high, a_low), (b_high, b_low) = a, b
    mm = functools.partial(jnp.dot, preferred_element_type=F32)
    return mm(a_high, b_high) + (mm(a_low, b_high) + mm(a_high, b_low))


def ends(first, last, length):
    scale = 1.0 / (1.0 - rho(2 * length))
    tail = rho(length)
    return (first + tail * last) * scale, (last + tail * first) * scale


def y_carry(tiles, edge):
    count = YT // 2
    heads = [jnp.broadcast_to(tiles[2 * b][:, 0:1], (8, LANES)) for b in range(count)]
    tails = [jnp.broadcast_to(tiles[2 * b + 1][:, LANES - 1:LANES], (8, LANES)) for b in range(count)]
    hop = rho(NB)
    right = [jnp.zeros_like(heads[0])]
    for b in range(count - 1):
        right.append(hop * right[-1] + tails[b])
    left = [jnp.zeros_like(heads[0])]
    for b in range(count - 1, 0, -1):
        left.append(hop * left[-1] + heads[b])
    left = left[::-1]
    from_low, from_high = ends(heads[0] + hop * left[0], tails[-1] + hop * right[-1], Y)
    out = []
    for b in range(count):
        carry_r = right[b] + rho(NB * b) * from_low
        carry_l = left[b] + rho(NB * (count - 1 - b)) * from_high
        for k in range(2):
            out.append(tiles[2 * b + k] + carry_r * edge[k:k + 1, :] + carry_l * edge[2 + k:3 + k, :])
    return out


MROWS = 16


def block_kernel(flag_ref, act_ref, c_hbm, l_hbm, xlo_ref, xhi_ref,
                 pot_hbm, u_hbm, mom_ref, edgepot_ref,
                 c_s, l_s, pot_s, u_s, st, hr, in_sem, pot_sem, u_sem):
    def copies_in(i):
        at = pl.ds(i * CHUNK, CHUNK)
        return (pltpu.make_async_copy(c_hbm.at[at], c_s.at[pl.ds(i * CHUNK + 3, CHUNK)], in_sem.at[0, i]),
                pltpu.make_async_copy(l_hbm.at[at], l_s.at[pl.ds(i * CHUNK + 3, CHUNK)], in_sem.at[1, i]))

    for i in range(NCHUNK):
        for copy in copies_in(i):
            copy.start()

    tile = (Z, LANES)
    sub, lane = sub_iota(tile), lane_iota(tile)
    top, first, last = sub == Z - 1, lane == 0, lane == LANES - 1
    WZ, WY, WX, BASE, REST, POT, SWEEP = range(7)

    def up_z(v):
        return pltpu.roll(v, Z - 1, 0)

    def down_z(v):
        return pltpu.roll(v, 1, 0)

    def up_y(v):
        return pltpu.roll(v, LANES - 1, 1)

    def down_y(v):
        return pltpu.roll(v, 1, 1)

    def ptile(e, t):
        return pl.ds(pl.multiple_of(e * ROW + t * Z, Z), Z)

    def advance(e, parity, open_x, inside):
        h = half_over_psi(l_s[e, 0])
        up_h, up_c = up_y(h), up_y(c_s[e, 0])
        below = below2 = jnp.zeros(tile, F32)
        held = None

        def second(t, pot1, up_pot, up_next, gx2, wz, wy, below2):
            gz = wz * (up_z(pot1) - pot1)
            gy = wy * (jnp.where(last, up_next, up_pot) - pot1)
            turned = down_y(gy)
            st[REST, t] = (gz - down_z(gz)) + (gy - jnp.where(first, below2, turned)) - gx2
            return turned

        for t in range(YT):
            c = c_s[e, t]
            if t + 1 < YT:
                h_next = half_over_psi(l_s[e, t + 1])
                up_h_next, up_c_next = up_y(h_next), up_y(c_s[e, t + 1])
            else:
                h_next, up_h_next, up_c_next = h, up_h, up_c
            h1 = hr[1 - parity, t]
            wx = recip(h1 + h) * open_x
            fx = wx * (c - c_s[e - 1, t])
            pot1 = st[BASE, t] - h1 * fx
            gx2 = st[WX, t] * (pot1 - st[POT, t])
            rhs = (act_ref[t] * inside) * (hr[parity, t] * (st[REST, t] + gx2))
            swept = RHO * st[SWEEP, t] + rhs
            u_s[e, t] = swept
            st[SWEEP, t] = swept
            st[POT, t] = pot1
            pot_s[ptile(e, t), :] = pot1
            wz_old, wy_old = st[WZ, t], st[WY, t]
            wz = jnp.where(top, 0.0, recip(h + up_z(h)))
            wy = recip(h + jnp.where(last, up_h_next, up_h))
            if t == YT - 1:
                wy = jnp.where(last, 0.0, wy)
            fz = wz * (up_z(c) - c)
            fy = wy * (jnp.where(last, up_c_next, up_c) - c)
            turned = down_y(fy)
            total = (fz - down_z(fz)) + (fy - jnp.where(first, below, turned)) - fx
            below = turned
            st[BASE, t] = c * (c * c - 1.0) - h * total
            st[WZ, t], st[WY, t], st[WX, t] = wz, wy, wx
            hr[parity, t] = h
            up_pot = up_y(pot1)
            if held is not None:
                t0, p0, u0, g0, z0, y0 = held
                below2 = second(t0, p0, u0, up_pot, g0, z0, y0, below2)
            held = (t, pot1, up_pot, gx2, wz_old, wy_old)
            h, up_h, up_c = h_next, up_h_next, up_c_next
        t0, p0, u0, g0, z0, y0 = held
        second(t0, p0, u0, u0, g0, z0, y0, below2)

    open_lo, open_hi = flag_ref[0], flag_ref[1]
    st[...] = jnp.zeros_like(st)
    hr[...] = jnp.ones_like(hr)
    c_s[0] = jnp.zeros((YT, Z, LANES), F32)
    for at, ref in ((1, xlo_ref), (X + 3, xhi_ref)):
        c_s[at:at + 2] = ref[0]
        l_s[at:at + 2] = ref[1].astype(jnp.int32)

    def pot_copy(i):
        src = pl.ds((i * CHUNK + 4) * ROW, CHUNK * ROW)
        return pltpu.make_async_copy(pot_s.at[src], pot_hbm.at[pl.ds(i * CHUNK * ROW, CHUNK * ROW)], pot_sem.at[i])

    pairs = CHUNK // 2

    def rows(j, _):
        turn = lax.rem(j, pairs) == 1

        @pl.when(jnp.logical_and(turn, j < X // 2))
        def _():
            for copy in copies_in((j - 1) // pairs):
                copy.wait()

        for parity in range(2):
            e = 2 * j + 1 + parity
            open_x = jnp.where(e <= 3, open_lo, jnp.where(e >= X + 3, open_hi, 1.0))
            advance(e, parity, open_x, jnp.where(e >= 5, 1.0, 0.0))

        @pl.when(jnp.logical_and(turn, j > pairs))
        def _():
            pot_copy((j - 1) // pairs - 1).start()
        return 0

    lax.fori_loop(0, X // 2 + 2, rows, 0)

    def u_copy(i):
        src = pl.ds(i * CHUNK + 5, CHUNK)
        return pltpu.make_async_copy(u_s.at[src], u_hbm.at[pl.ds(i * CHUNK, CHUNK)], u_sem.at[i])

    def back(k, carry):
        x = X - 1 - k
        mine, after = carry
        before = u_s[x + 4]
        u_s[x + 5] = GAIN * (mine + after)

        @pl.when(lax.rem(x, CHUNK) == 0)
        def _():
            u_copy(x // CHUNK).start()
        return before, RHO * (after + (mine - RHO * before))

    lax.fori_loop(0, X, back, (u_s[X + 4], jnp.zeros((YT, Z, LANES), F32)))
    mom_ref[0] = u_s[X + 4]
    mom_ref[1] = u_s[5]
    for side, z in ((0, 0), (1, 7)):
        edgepot_ref[side] = pot_s[pl.ds(4 * ROW + z, FACE, stride=Z), :]

    for i in range(NCHUNK):
        pot_copy(i).wait()
        u_copy(i).wait()


def solve_block(flags, act, c, level, xlo, xhi):
    any_spec = pl.BlockSpec(memory_space=pltpu.HBM)
    vm = pl.BlockSpec(memory_space=pltpu.VMEM)
    sm = pl.BlockSpec(memory_space=pltpu.SMEM)
    block = (X, YT, Z, LANES)
    return pl.pallas_call(
        block_kernel,
        in_specs=[sm, sm, any_spec, any_spec, vm, vm],
        out_specs=[any_spec, any_spec, vm, vm],
        out_shape=[
            jax.ShapeDtypeStruct((ROWS, LANES), F32),
            jax.ShapeDtypeStruct(block, F32),
            jax.ShapeDtypeStruct((2, YT, Z, LANES), F32),
            jax.ShapeDtypeStruct((2, FACE, LANES), F32),
        ],
        scratch_shapes=[
            pltpu.VMEM((X + 5, YT, Z, LANES), F32),
            pltpu.VMEM((X + 5, YT, Z, LANES), jnp.int32),
            pltpu.VMEM(((X + 5) * ROW, LANES), F32),
            pltpu.VMEM((X + 5, YT, Z, LANES), F32),
            pltpu.VMEM((7, YT, Z, LANES), F32),
            pltpu.VMEM((2, YT, Z, LANES), F32),
            pltpu.SemaphoreType.DMA((2, NCHUNK)),
            pltpu.SemaphoreType.DMA((NCHUNK,)),
            pltpu.SemaphoreType.DMA((NCHUNK,)),
        ],
        compiler_params=vmem(60),
        cost_estimate=pl.CostEstimate(flops=4 * 10**9, bytes_accessed=60 * 2**20, transcendentals=0),
        name="block",
    )(flags, act, c.reshape(block), level.reshape(block), xlo, xhi)


EXT = X + 2
GROUP = 8


def seam_kernel(flag_ref, pow_ref, own_lo, own_hi, inner_hbm, got_lo, got_hi, xlo_ref, xhi_ref,
                corner_lo_ref, corner_hi_ref, edgepot_hbm, mom_ref, act_ref,
                df_hbm, dpot_hbm, send_ref, ext_s, in_s, df_s, dpot_s, fl_s, acc_s, in_sem, out_sem):
    open_x = (flag_ref[0], flag_ref[1])
    tile_row = lax.broadcasted_iota(jnp.int32, (YT, LANES), 0)
    act = jnp.zeros((YT, LANES), F32)
    for t in range(YT):
        act = jnp.where(tile_row == t, act_ref[t], act)
    shape = (GROUP, YT, LANES)
    open_y = jnp.logical_or(
        lax.broadcasted_iota(jnp.int32, shape, 2) < LANES - 1,
        lax.broadcasted_iota(jnp.int32, shape, 1) < YT - 1,
    )
    row = lax.broadcasted_iota(jnp.int32, shape, 0)
    acc_s[...] = jnp.zeros_like(acc_s)
    main = pl.ds(1, X)

    def arrivals(side):
        own, got = ((own_lo, got_lo), (own_hi, got_hi))[side]
        pairs = [(own.at[0], ext_s.at[side, 0, main]), (own.at[1], ext_s.at[side, 1, main]),
                 (got.at[0], ext_s.at[side, 2, main]), (got.at[1], ext_s.at[side, 3, main]),
                 (got.at[2], in_s.at[side, 0]), (inner_hbm.at[side], in_s.at[side, 1]),
                 (edgepot_hbm.at[side], in_s.at[side, 2])]
        return [pltpu.make_async_copy(far, near, in_sem.at[side, k]) for k, (far, near) in enumerate(pairs)]

    def departures(side):
        at = pl.ds(2 * side, 2)
        return [pltpu.make_async_copy(df_s.at[at], df_hbm.at[at], out_sem.at[side, 0]),
                pltpu.make_async_copy(dpot_s.at[side], dpot_hbm.at[side], out_sem.at[side, 1])]

    for side in range(2):
        for copy in arrivals(side):
            copy.start()

    for side, (corner, z) in enumerate(((corner_lo_ref, 0), (corner_hi_ref, 7))):
        for spot, ref, r, k in ((0, xlo_ref, 1, 0), (EXT - 1, xhi_ref, 0, 1)):
            ext_s[side, 0, spot] = ref[0, r, :, z, :]
            ext_s[side, 1, spot] = half_over_psi(ref[1, r, :, z, :])
            ext_s[side, 2, spot] = corner[2 * k]
            ext_s[side, 3, spot] = half_over_psi(corner[2 * k + 1])

    def one_side(side, _):
        for k in range(2):
            @pl.when(side == k)
            def _():
                for copy in arrivals(k):
                    copy.wait()
        open_z = flag_ref[2 + side]
        bias = 1.0 - open_z
        c0_s, h0_s, cm_s, hm_s, dp_s = (ext_s.at[side, k] for k in range(5))
        got2_s, inner_s, pot_s = (in_s.at[side, k] for k in range(3))

        def first(i, _):
            at = pl.ds(i * 6, 6)
            h0 = h0_s[at]
            flux = recip(h0 + hm_s[at]) * open_z * (cm_s[at] - c0_s[at])
            fl_s[at] = flux
            dp_s[at] = -h0 * flux
            return 0

        lax.fori_loop(0, EXT // 6, first, 0)

        def second(i, _):
            at = pl.ds(i * GROUP, GROUP)
            ext = pl.ds(i * GROUP + 1, GROUP)
            after = pl.ds(i * GROUP + 2, GROUP)
            lo_gate = jnp.where(row == 0, jnp.where(i == 0, open_x[0], 1.0), 1.0)
            hi_gate = jnp.where(row == GROUP - 1, jnp.where(i == X // GROUP - 1, open_x[1], 1.0), 1.0)

            def plane(h_ref, v_ref, extra):
                h, v = h_ref[ext] + extra, v_ref[ext]
                wy = jnp.where(open_y, recip(h + next_y(h)), 0.0)
                fy = wy * (next_y(v) - v)
                total = recip(h + h_ref[at]) * lo_gate * (v_ref[at] - v)
                total = total + recip(h + h_ref[after]) * hi_gate * (v_ref[after] - v)
                return h, v, total + (fy - prev_y(fy))

            hm, cm, across_m = plane(hm_s, cm_s, bias)
            h0, dp, across_0 = plane(h0_s, dp_s, 0.0)
            flux = fl_s[ext]
            potm = cm * (cm * cm - 1.0) - hm * (across_m + got2_s[at] - flux)
            pot0 = pot_s[at] + dp
            h1 = inner_s[at]
            toward = recip(h0 + h1) * dp
            join = recip(h0 + hm) * open_z * (potm - pot0)
            df0 = act * (h0 * (across_0 - toward + join))
            df1 = act * (h1 * toward)
            outer, inner = 3 * side, 1 + side
            df_s[outer, at] = df0
            df_s[inner, at] = df1
            dpot_s[side, at] = dp
            for spot, value in ((outer, df0), (inner, df1)):
                last, start = acc_s[spot], acc_s[4 + spot]
                for r in range(GROUP):
                    x = i * GROUP + r
                    last = last + pow_ref[1, X - 1 - x] * value[r]
                    start = start + pow_ref[1, x] * value[r]
                acc_s[spot] = last
                acc_s[4 + spot] = start
            return 0

        lax.fori_loop(0, X // GROUP, second, 0)
        for copy in departures(side):
            copy.start()
        return 0

    lax.fori_loop(0, 2, one_side, 0)

    sub = sub_iota((Z, LANES))
    half = sub < 4
    for t in range(YT):
        totals = []
        for which in range(2):
            total = mom_ref[which, t]
            for k, z in enumerate((0, 1, 6, 7)):
                line = jnp.broadcast_to(acc_s[4 * which + k, t:t + 1, :], (Z, LANES))
                total = total + jnp.where(sub == z, line, 0.0)
            totals.append(total)
        last, start = totals
        send_ref[2 * t] = jnp.where(half, last, pltpu.roll(start, 4, 0))
        send_ref[2 * t + 1] = jnp.where(half, pltpu.roll(last, 4, 0), start)
    for side in range(2):
        for copy in departures(side):
            copy.wait()


def add_seams(flags, powers, own_lo, own_hi, inner, got_lo, got_hi, xlo, xhi, corner_lo, corner_hi, edgepot, mom, act):
    vm = pl.BlockSpec(memory_space=pltpu.VMEM)
    sm = pl.BlockSpec(memory_space=pltpu.SMEM)
    hbm = pl.BlockSpec(memory_space=pltpu.HBM)
    lines = [a.reshape(a.shape[0], X, YT, LANES) for a in (own_lo, own_hi, inner, got_lo, got_hi)]
    return pl.pallas_call(
        seam_kernel,
        in_specs=[sm, sm] + [hbm] * 5 + [vm] * 4 + [hbm, vm, sm],
        out_specs=[hbm, hbm, vm],
        out_shape=[
            jax.ShapeDtypeStruct((4, X, YT, LANES), F32),
            jax.ShapeDtypeStruct((2, X, YT, LANES), F32),
            jax.ShapeDtypeStruct((32, Z, LANES), F32),
        ],
        scratch_shapes=[
            pltpu.VMEM((2, 5, EXT, YT, LANES), F32),
            pltpu.VMEM((2, 3, X, YT, LANES), F32),
            pltpu.VMEM((4, X, YT, LANES), F32),
            pltpu.VMEM((2, X, YT, LANES), F32),
            pltpu.VMEM((EXT, YT, LANES), F32),
            pltpu.VMEM((8, YT, LANES), F32),
            pltpu.SemaphoreType.DMA((2, 7)),
            pltpu.SemaphoreType.DMA((2, 2)),
        ],
        compiler_params=vmem(60),
        cost_estimate=pl.CostEstimate(flops=10**7, bytes_accessed=12 * 2**20, transcendentals=0),
        name="seams",
    )(flags, powers, *lines, xlo, xhi, corner_lo, corner_hi, edgepot.reshape(2, X, YT, LANES), mom, act)


def settle_kernel(pot_hbm, u_hbm, dpot_ref, df_ref, pot_out, u_out, pot_s, u_s, p_s, in_sem, out_sem):
    def moves(i):
        at = pl.ds(i * CHUNK * ROW, CHUNK * ROW)
        return [
            (pltpu.make_async_copy(far.at[at], near.at[at], in_sem.at[k, i]),
             pltpu.make_async_copy(near.at[at], out.at[at], out_sem.at[k, i]))
            for k, (far, near, out) in enumerate(((pot_hbm, pot_s, pot_out), (u_hbm, u_s, u_out)))
        ]

    for i in reversed(range(NCHUNK)):
        for start, _ in moves(i):
            start.start()

    shape = (4, YT, LANES)

    def forth(x, carry):
        carry = RHO * carry + df_ref[:, x]
        p_s[:, x] = carry
        return carry

    lax.fori_loop(0, X, forth, jnp.zeros(shape, F32), unroll=8)

    def back(k, carry):
        x = X - 1 - k
        solved = GAIN * (p_s[:, x] + carry)
        for n, z in enumerate((0, 1, 6, 7)):
            at = pl.ds(x * ROW + z, YT, stride=Z)
            u_s[at, :] = u_s[at, :] + solved[n]
        return RHO * (carry + df_ref[:, x])

    def chunk(done, carry):
        i = NCHUNK - 1 - done
        (pot_in, pot_back), (u_in, u_back) = moves(i)
        pot_in.wait()
        for side, z in ((0, 0), (1, 7)):
            at = pl.ds(i * CHUNK * ROW + z, PART, stride=Z)
            pot_s[at, :] = pot_s[at, :] + dpot_ref[side, pl.ds(i * PART, PART), :]
        pot_back.start()
        u_in.wait()
        carry = lax.fori_loop(0, CHUNK, lambda k, c: back(done * CHUNK + k, c), carry, unroll=4)
        u_back.start()
        return carry

    lax.fori_loop(0, NCHUNK, chunk, jnp.zeros(shape, F32))
    for i in range(NCHUNK):
        for _, back_copy in moves(i):
            back_copy.wait()


def settle(pot, u, dpot, df):
    vm = pl.BlockSpec(memory_space=pltpu.VMEM)
    any_spec = pl.BlockSpec(memory_space=pltpu.HBM)
    rows = jax.ShapeDtypeStruct((ROWS, LANES), F32)
    return pl.pallas_call(
        settle_kernel,
        in_specs=[any_spec, any_spec, vm, vm],
        out_specs=[any_spec, any_spec],
        out_shape=[rows, rows],
        scratch_shapes=[
            pltpu.VMEM((ROWS, LANES), F32),
            pltpu.VMEM((ROWS, LANES), F32),
            pltpu.VMEM((4, X, YT, LANES), F32),
            pltpu.SemaphoreType.DMA((2, NCHUNK)),
            pltpu.SemaphoreType.DMA((2, NCHUNK)),
        ],
        compiler_params=vmem(60),
        cost_estimate=pl.CostEstimate(flops=10**7, bytes_accessed=10 * 2**20, transcendentals=0),
        name="settle",
    )(pot, u.reshape(ROWS, LANES), dpot.reshape(2, FACE, LANES), df)


def lines_kernel(u_hbm, thigh_ref, tlow_ref, edge_ref, out_hbm, u_s, w_s, in_sem, out_sem):
    groups = X // MROWS

    def moves(i):
        at = pl.ds(i * MROWS, MROWS)
        return (pltpu.make_async_copy(u_hbm.at[at], u_s.at[at], in_sem.at[i]),
                pltpu.make_async_copy(u_s.at[at], out_hbm.at[at], out_sem.at[i]))

    for i in range(groups):
        moves(i)[0].start()
    edge = edge_ref[...]

    def group(i, _):
        come, leave = moves(i)
        come.wait()
        xs = pl.ds(i * MROWS, MROWS)
        table = (thigh_ref[...], tlow_ref[...])
        for b in range(YT // 2):
            pair = [u_s[xs, 2 * b + k].reshape(MROWS * Z, LANES) for k in range(2)]
            solved = dot3(split(jnp.concatenate(pair, axis=1)), table)
            for k in range(2):
                w_s[:, 2 * b + k] = solved[:, k * LANES:(k + 1) * LANES].reshape(MROWS, Z, LANES)

        def body(x, _):
            for t, part in enumerate(y_carry([w_s[x, t] for t in range(YT)], edge)):
                u_s[i * MROWS + x, t] = part
            return 0

        lax.fori_loop(0, MROWS, body, 0, unroll=UNROLL)
        leave.start()
        return 0

    lax.fori_loop(0, groups, group, 0)
    for i in range(groups):
        moves(i)[1].wait()


UNROLL = 4


def solve_lines(u, tables):
    vm = pl.BlockSpec(memory_space=pltpu.VMEM)
    hbm = pl.BlockSpec(memory_space=pltpu.HBM)
    return pl.pallas_call(
        lines_kernel,
        in_specs=[hbm] + [vm] * 3,
        out_specs=hbm,
        out_shape=jax.ShapeDtypeStruct((X, YT, Z, LANES), F32),
        scratch_shapes=[
            pltpu.VMEM((X, YT, Z, LANES), F32),
            pltpu.VMEM((MROWS, YT, Z, LANES), F32),
            pltpu.SemaphoreType.DMA((X // MROWS,)),
            pltpu.SemaphoreType.DMA((X // MROWS,)),
        ],
        compiler_params=vmem(60),
        cost_estimate=pl.CostEstimate(flops=2 * 10**9, bytes_accessed=10 * 2**20, transcendentals=0),
        name="lines",
    )(u, *tables)


def carries_kernel(count, in_ref, out_ref):
    got = [in_ref[d] for d in range(count)]
    half = sub_iota((8, TILE)) < 4
    hop = rho(X)
    right = [jnp.zeros((8, TILE), F32)]
    for d in range(count - 1):
        right.append(hop * right[-1] + got[d])
    starts = [pltpu.roll(g, 4, 0) for g in got]
    left = [jnp.zeros((8, TILE), F32)]
    for d in range(count - 1, 0, -1):
        left.append(hop * left[-1] + starts[d])
    left = left[::-1]
    from_low, from_high = ends(starts[0] + hop * left[0], got[-1] + hop * right[-1], X * count)
    for d in range(count):
        carry_r = right[d] + rho(X * d) * from_low
        carry_l = left[d] + rho(X * (count - 1 - d)) * from_high
        out_ref[d] = jnp.where(half, carry_r, pltpu.roll(carry_l, 4, 0))


def scan_carries(got):
    vm = pl.BlockSpec(memory_space=pltpu.VMEM)
    return pl.pallas_call(
        functools.partial(carries_kernel, got.shape[0]),
        in_specs=[vm],
        out_specs=vm,
        out_shape=jax.ShapeDtypeStruct(got.shape, F32),
        cost_estimate=pl.CostEstimate(flops=10**6, bytes_accessed=2**18, transcendentals=0),
        name="carries",
    )(got)


FIN = 8


def final_kernel(pow_ref, got_ref, thigh_ref, tlow_ref, edge_ref, v_hbm, out_hbm, v_s, lr_s, in_sem, out_sem):
    def moves(i):
        at = pl.ds(i * FIN * ROW, FIN * ROW)
        return (pltpu.make_async_copy(v_hbm.at[at], v_s.at[at], in_sem.at[i]),
                pltpu.make_async_copy(v_s.at[at], out_hbm.at[at], out_sem.at[i]))

    for i in range(X // FIN):
        moves(i)[0].start()
    half = sub_iota((Z, LANES)) < 4
    edge = edge_ref[...]

    def solve(b, _):
        pair = []
        for k in range(2):
            even, odd = got_ref[4 * b + 2 * k], got_ref[4 * b + 2 * k + 1]
            pair.append(jnp.concatenate([
                jnp.where(half, even, pltpu.roll(odd, 4, 0)),
                jnp.where(half, pltpu.roll(even, 4, 0), odd),
            ], axis=0))
        solved = dot3(split(jnp.concatenate(pair, axis=1)), (thigh_ref[...], tlow_ref[...]))
        for side in range(2):
            for k in range(2):
                lr_s[side, 2 * b + k] = solved[8 * side:8 * side + 8, k * LANES:(k + 1) * LANES]
        return 0

    lax.fori_loop(0, YT // 2, solve, 0)

    def carry(side, _):
        for t, part in enumerate(y_carry([lr_s[side, t] for t in range(YT)], edge)):
            lr_s[side, t] = part
        return 0

    lax.fori_loop(0, 2, carry, 0)

    def chunk(i, _):
        come, leave = moves(i)
        come.wait()

        def row(r, _):
            x = i * FIN + r
            at = pl.ds(pl.multiple_of(x * ROW, ROW), ROW)
            low, high = (lr_s[side].reshape(ROW, LANES) for side in range(2))
            v_s[at, :] = v_s[at, :] + pow_ref[0, x] * low + pow_ref[0, X - 1 - x] * high
            return 0

        lax.fori_loop(0, FIN, row, 0, unroll=2)
        leave.start()
        return 0

    lax.fori_loop(0, X // FIN, chunk, 0)
    for i in range(X // FIN):
        moves(i)[1].wait()


def finish(powers, got, tables, v):
    vm = pl.BlockSpec(memory_space=pltpu.VMEM)
    hbm = pl.BlockSpec(memory_space=pltpu.HBM)
    return pl.pallas_call(
        final_kernel,
        in_specs=[pl.BlockSpec(memory_space=pltpu.SMEM)] + [vm] * 4 + [hbm],
        out_specs=hbm,
        out_shape=jax.ShapeDtypeStruct((ROWS, LANES), F32),
        scratch_shapes=[
            pltpu.VMEM((ROWS, LANES), F32),
            pltpu.VMEM((2, YT, Z, LANES), F32),
            pltpu.SemaphoreType.DMA((X // FIN,)),
            pltpu.SemaphoreType.DMA((X // FIN,)),
        ],
        compiler_params=vmem(60),
        cost_estimate=pl.CostEstimate(flops=10**7, bytes_accessed=10 * 2**20, transcendentals=0),
        name="finish",
    )(powers, got, *tables, v)


def shift(value, axis, forward):
    count = lax.axis_size(axis)
    pairs = [(i, i + 1) for i in range(count - 1)]
    if not forward:
        pairs = [(b, a) for a, b in pairs]
    return lax.ppermute(value, axis, pairs)


def to_tiles(block):
    return block.reshape(X, Z, YT, LANES).transpose(0, 2, 1, 3).reshape(ROWS, LANES)


def from_tiles(rows):
    return rows.reshape(X, YT, Z, LANES).transpose(0, 2, 1, 3).reshape(X, Z, Y)


def per_device(concentration, psi_level, tile_mask):
    c, level = to_tiles(concentration), to_tiles(psi_level)
    xy, gz = lax.axis_index("xy"), lax.axis_index("gz")
    n_xy, n_gz = lax.axis_size("xy"), lax.axis_size("gz")
    flags = jnp.stack([xy > 0, xy < n_xy - 1, gz > 0, gz < n_gz - 1]).astype(F32)
    mask_row = lax.dynamic_index_in_dim(tile_mask, xy * X // TILE, 0, keepdims=False)
    act = mask_row.astype(F32) * (2.0 * TIME_STEP)
    tables = tuple(jnp.asarray(t) for t in y_tables())
    steps = np.exp(-THETA * np.arange(X + 1))
    powers = jnp.asarray(np.stack([steps[1:], GAIN * steps[:-1]]).astype(np.float32))

    zlo, zhi, inner, xlo, xhi = make_faces(c, level)
    pair = (2, 2, YT, Z, LANES)
    got_xlo = shift(xhi, "xy", True).reshape(pair)
    got_xhi = shift(xlo, "xy", False).reshape(pair)
    got_zlo = shift(zhi, "gz", True)
    got_zhi = shift(zlo, "gz", False)

    def corners(z):
        return jnp.stack([got_xlo[0, 1, :, z], got_xlo[1, 1, :, z], got_xhi[0, 0, :, z], got_xhi[1, 0, :, z]])

    corner_lo = shift(corners(7), "gz", True)
    corner_hi = shift(corners(0), "gz", False)

    pot, u, mom, edgepot = solve_block(flags, act, c, level, got_xlo, got_xhi)
    df, dpot, send = add_seams(
        flags, powers, zlo, zhi, inner, got_zlo, got_zhi, got_xlo, got_xhi, corner_lo, corner_hi, edgepot, mom, act,
    )
    got = lax.all_to_all(send, "xy", split_axis=0, concat_axis=0, tiled=True)
    potential, u = settle(pot, u, dpot, df)
    got, u = lax.optimization_barrier((got, u))
    back = lax.all_to_all(scan_carries(got), "xy", split_axis=0, concat_axis=0, tiled=True)
    v = solve_lines(u.reshape(X, YT, Z, LANES), tables)
    increment = finish(powers, back, tables, v.reshape(ROWS, LANES))
    return from_tiles(potential), from_tiles(increment)


def solution(mesh):
    placed = (P("xy", "gz", None), P("xy", "gz", None), P())
    return jax.shard_map(
        per_device,
        mesh=mesh,
        in_specs=placed,
        out_specs=(P("xy", "gz", None), P("xy", "gz", None)),
        check_vma=False,
    )
```

```python
import functools
import math

import jax
import jax.numpy as jnp
import numpy as np
from jax import lax
from jax.experimental import pallas as pl
from jax.experimental.pallas import tpu as pltpu
from jax.sharding import PartitionSpec as P

TILE = 128
LEVELS = 4096
STIFF = 4096
GRADIENT_COEF = 0.5
TIME_STEP = 32.0
PSI_FLOOR = 0.25

X = 64
Z = 8
Y = 2048
YT = 16
LANES = 128
ROW = YT * Z
ROWS = X * ROW
FACE = X * YT
LINE = 2048
NB = 256
F32 = jnp.float32
BF16 = jnp.bfloat16

_half = 1.0 + 0.5 / STIFF
THETA = math.log(_half + math.sqrt(_half * _half - 1.0))
RHO = math.exp(-THETA)
GAIN = (RHO / STIFF) / (1.0 - RHO * RHO)


def rho(power):
    return math.exp(-THETA * power)


def vmem(limit_mib):
    return pltpu.CompilerParams(vmem_limit_bytes=limit_mib * 2**20)


def half_over_psi(level):
    return recip(2.0 * PSI_FLOOR + level.astype(F32) * (2.0 * (1.0 - PSI_FLOOR) / (LEVELS - 1)))


def recip(value):
    return pl.reciprocal(value, approx=True)


def lane_iota(shape):
    return lax.broadcasted_iota(jnp.int32, shape, len(shape) - 1)


def sub_iota(shape):
    return lax.broadcasted_iota(jnp.int32, shape, len(shape) - 2)


def next_y(v):
    axis = v.ndim - 1
    turned = pltpu.roll(v, LANES - 1, axis)
    if TILES_LEAD[v.shape[-2]]:
        following = jnp.concatenate([turned[1:], turned[:1]], axis=0)
    else:
        following = pltpu.roll(turned, YT - 1, axis - 1)
    return jnp.where(lane_iota(v.shape) == LANES - 1, following, turned)


def prev_y(v):
    axis = v.ndim - 1
    turned = pltpu.roll(v, 1, axis)
    if TILES_LEAD[v.shape[-2]]:
        previous = jnp.concatenate([turned[-1:], turned[:-1]], axis=0)
    else:
        previous = pltpu.roll(turned, 1, axis - 1)
    return jnp.where(lane_iota(v.shape) == 0, previous, turned)


TILES_LEAD = {Z: True, YT: False}


def next_z(v):
    return pltpu.roll(v, Z - 1, 1)


def prev_z(v):
    return pltpu.roll(v, 1, 1)


CHUNK = 8
NCHUNK = X // CHUNK
PART = CHUNK * YT


def faces_kernel(c_hbm, l_hbm, zlo_hbm, zhi_hbm, in_hbm, xlo_ref, xhi_ref, c_s, l_s, z_s, i_s, in_sem, out_sem):
    def arrivals(i):
        at = pl.ds(i * CHUNK * ROW, CHUNK * ROW)
        return (pltpu.make_async_copy(c_hbm.at[at], c_s.at[at], in_sem.at[0, i]),
                pltpu.make_async_copy(l_hbm.at[at], l_s.at[at], in_sem.at[1, i]))

    def departures(i):
        at = pl.ds(i * PART, PART)
        pairs = ((z_s.at[0, :, at], zlo_hbm.at[:, at]), (z_s.at[1, :, at], zhi_hbm.at[:, at]),
                 (i_s.at[:, at], in_hbm.at[:, at]))
        return [pltpu.make_async_copy(near, far, out_sem.at[k, i]) for k, (near, far) in enumerate(pairs)]

    for i in range(NCHUNK):
        for copy in arrivals(i):
            copy.start()

    def chunk(i, _):
        for copy in arrivals(i):
            copy.wait()
        out = pl.ds(i * PART, PART)

        def plane(ref, z):
            return ref[pl.ds(i * CHUNK * ROW + z, PART, stride=Z), :]

        for side, edge, inner in ((0, 0, 1), (1, 7, 6)):
            c_edge, c_inner = plane(c_s, edge), plane(c_s, inner)
            h_edge = half_over_psi(plane(l_s, edge))
            h_inner = half_over_psi(plane(l_s, inner))
            z_s[side, 0, out] = c_edge
            z_s[side, 1, out] = h_edge
            z_s[side, 2, out] = recip(h_edge + h_inner) * (c_inner - c_edge)
            i_s[side, out] = h_inner
        for copy in departures(i):
            copy.start()
        return 0

    lax.fori_loop(0, NCHUNK, chunk, 0)
    last = (X - 2) * ROW
    for ref, at in ((xlo_ref, 0), (xhi_ref, last)):
        ref[0] = c_s[at:at + 2 * ROW, :]
        ref[1] = l_s[at:at + 2 * ROW, :].astype(F32)
    for i in range(NCHUNK):
        for copy in departures(i):
            copy.wait()


def make_faces(c, level):
    hbm = pl.BlockSpec(memory_space=pltpu.HBM)
    vm = pl.BlockSpec(memory_space=pltpu.VMEM)
    return pl.pallas_call(
        faces_kernel,
        in_specs=[hbm, hbm],
        out_specs=[hbm, hbm, hbm, vm, vm],
        out_shape=[
            jax.ShapeDtypeStruct((3, FACE, LANES), F32),
            jax.ShapeDtypeStruct((3, FACE, LANES), F32),
            jax.ShapeDtypeStruct((2, FACE, LANES), F32),
            jax.ShapeDtypeStruct((2, 2 * ROW, LANES), F32),
            jax.ShapeDtypeStruct((2, 2 * ROW, LANES), F32),
        ],
        scratch_shapes=[
            pltpu.VMEM((ROWS, LANES), F32),
            pltpu.VMEM((ROWS, LANES), jnp.int32),
            pltpu.VMEM((2, 3, FACE, LANES), F32),
            pltpu.VMEM((2, FACE, LANES), F32),
            pltpu.SemaphoreType.DMA((2, NCHUNK)),
            pltpu.SemaphoreType.DMA((3, NCHUNK)),
        ],
        compiler_params=vmem(50),
        cost_estimate=pl.CostEstimate(flops=10**6, bytes_accessed=13 * 2**20, transcendentals=0),
        name="faces",
    )(c, level)


def y_tables():
    idx = np.arange(NB)
    table = GAIN * np.exp(-THETA * np.abs(idx[:, None] - idx[None, :]))
    high = table.astype(jnp.bfloat16)
    low = (table - high.astype(np.float64)).astype(jnp.bfloat16)
    fwd = np.exp(-THETA * (idx + 1.0))
    bwd = np.exp(-THETA * (NB - idx.astype(np.float64)))
    edge = np.zeros((8, LANES), np.float32)
    edge[0], edge[1] = fwd[:LANES], fwd[LANES:]
    edge[2], edge[3] = bwd[:LANES], bwd[LANES:]
    return high, low, edge


def split(v):
    high = v.astype(BF16)
    return high, (v - high.astype(F32)).astype(BF16)


def dot3(a, b):
    (a_high, a_low), (b_high, b_low) = a, b
    mm = functools.partial(jnp.dot, preferred_element_type=F32)
    both = mm(jnp.concatenate([a_high, a_low], axis=0), b_high)
    rows = a_high.shape[0]
    return both[:rows] + (both[rows:] + mm(a_high, b_low))


def ends(first, last, length):
    scale = 1.0 / (1.0 - rho(2 * length))
    tail = rho(length)
    return (first + tail * last) * scale, (last + tail * first) * scale


def y_carry(tiles, edge):
    count = YT // 2
    heads = [jnp.broadcast_to(tiles[2 * b][:, 0:1], (8, LANES)) for b in range(count)]
    tails = [jnp.broadcast_to(tiles[2 * b + 1][:, LANES - 1:LANES], (8, LANES)) for b in range(count)]
    hop = rho(NB)
    right = [jnp.zeros_like(heads[0])]
    for b in range(count - 1):
        right.append(hop * right[-1] + tails[b])
    left = [jnp.zeros_like(heads[0])]
    for b in range(count - 1, 0, -1):
        left.append(hop * left[-1] + heads[b])
    left = left[::-1]
    from_low, from_high = ends(heads[0] + hop * left[0], tails[-1] + hop * right[-1], Y)
    out = []
    for b in range(count):
        carry_r = right[b] + rho(NB * b) * from_low
        carry_l = left[b] + rho(NB * (count - 1 - b)) * from_high
        for k in range(2):
            out.append(tiles[2 * b + k] + carry_r * edge[k:k + 1, :] + carry_l * edge[2 + k:3 + k, :])
    return out


MROWS = 16


def block_kernel(flag_ref, act_ref, c_hbm, l_hbm, xlo_ref, xhi_ref,
                 pot_hbm, u_hbm, mom_ref, edgepot_ref,
                 c_s, l_s, pot_s, u_s, st, hr, in_sem, pot_sem, u_sem):
    def copies_in(i):
        at = pl.ds(i * CHUNK, CHUNK)
        return (pltpu.make_async_copy(c_hbm.at[at], c_s.at[pl.ds(i * CHUNK + 3, CHUNK)], in_sem.at[0, i]),
                pltpu.make_async_copy(l_hbm.at[at], l_s.at[pl.ds(i * CHUNK + 3, CHUNK)], in_sem.at[1, i]))

    for i in range(NCHUNK):
        for copy in copies_in(i):
            copy.start()

    tile = (Z, LANES)
    sub, lane = sub_iota(tile), lane_iota(tile)
    top, first, last = sub == Z - 1, lane == 0, lane == LANES - 1
    WZ, WY, WX, BASE, REST, POT, SWEEP = range(7)

    def up_z(v):
        return pltpu.roll(v, Z - 1, 0)

    def down_z(v):
        return pltpu.roll(v, 1, 0)

    def up_y(v):
        return pltpu.roll(v, LANES - 1, 1)

    def down_y(v):
        return pltpu.roll(v, 1, 1)

    def ptile(e, t):
        return pl.ds(pl.multiple_of(e * ROW + t * Z, Z), Z)

    def advance(e, parity, open_x, inside):
        h = half_over_psi(l_s[e, 0])
        up_h, up_c = up_y(h), up_y(c_s[e, 0])
        below = below2 = jnp.zeros(tile, F32)
        held = None

        def second(t, pot1, up_pot, up_next, gx2, wz, wy, below2):
            gz = wz * (up_z(pot1) - pot1)
            gy = wy * (jnp.where(last, up_next, up_pot) - pot1)
            turned = down_y(gy)
            st[REST, t] = (gz - down_z(gz)) + (gy - jnp.where(first, below2, turned)) - gx2
            return turned

        for t in range(YT):
            c = c_s[e, t]
            if t + 1 < YT:
                h_next = half_over_psi(l_s[e, t + 1])
                up_h_next, up_c_next = up_y(h_next), up_y(c_s[e, t + 1])
            else:
                h_next, up_h_next, up_c_next = h, up_h, up_c
            h1 = hr[1 - parity, t]
            wx = recip(h1 + h) * open_x
            fx = wx * (c - c_s[e - 1, t])
            pot1 = st[BASE, t] - h1 * fx
            gx2 = st[WX, t] * (pot1 - st[POT, t])
            rhs = (act_ref[t] * inside) * (hr[parity, t] * (st[REST, t] + gx2))
            swept = RHO * st[SWEEP, t] + rhs
            u_s[e, t] = swept
            st[SWEEP, t] = swept
            st[POT, t] = pot1
            pot_s[ptile(e, t), :] = pot1
            wz_old, wy_old = st[WZ, t], st[WY, t]
            wz = jnp.where(top, 0.0, recip(h + up_z(h)))
            wy = recip(h + jnp.where(last, up_h_next, up_h))
            if t == YT - 1:
                wy = jnp.where(last, 0.0, wy)
            fz = wz * (up_z(c) - c)
            fy = wy * (jnp.where(last, up_c_next, up_c) - c)
            turned = down_y(fy)
            total = (fz - down_z(fz)) + (fy - jnp.where(first, below, turned)) - fx
            below = turned
            st[BASE, t] = c * (c * c - 1.0) - h * total
            st[WZ, t], st[WY, t], st[WX, t] = wz, wy, wx
            hr[parity, t] = h
            up_pot = up_y(pot1)
            if held is not None:
                t0, p0, u0, g0, z0, y0 = held
                below2 = second(t0, p0, u0, up_pot, g0, z0, y0, below2)
            held = (t, pot1, up_pot, gx2, wz_old, wy_old)
            h, up_h, up_c = h_next, up_h_next, up_c_next
        t0, p0, u0, g0, z0, y0 = held
        second(t0, p0, u0, u0, g0, z0, y0, below2)

    open_lo, open_hi = flag_ref[0], flag_ref[1]
    st[...] = jnp.zeros_like(st)
    hr[...] = jnp.ones_like(hr)
    c_s[0] = jnp.zeros((YT, Z, LANES), F32)
    for at, ref in ((1, xlo_ref), (X + 3, xhi_ref)):
        c_s[at:at + 2] = ref[0]
        l_s[at:at + 2] = ref[1].astype(jnp.int32)

    def pot_copy(i):
        src = pl.ds((i * CHUNK + 4) * ROW, CHUNK * ROW)
        return pltpu.make_async_copy(pot_s.at[src], pot_hbm.at[pl.ds(i * CHUNK * ROW, CHUNK * ROW)], pot_sem.at[i])

    pairs = CHUNK // 2

    def rows(j, _):
        turn = lax.rem(j, pairs) == 1

        @pl.when(jnp.logical_and(turn, j < X // 2))
        def _():
            for copy in copies_in((j - 1) // pairs):
                copy.wait()

        for parity in range(2):
            e = 2 * j + 1 + parity
            open_x = jnp.where(e <= 3, open_lo, jnp.where(e >= X + 3, open_hi, 1.0))
            advance(e, parity, open_x, jnp.where(e >= 5, 1.0, 0.0))

        @pl.when(jnp.logical_and(turn, j > pairs))
        def _():
            pot_copy((j - 1) // pairs - 1).start()
        return 0

    lax.fori_loop(0, X // 2 + 2, rows, 0)

    def u_copy(i):
        src = pl.ds(i * CHUNK + 5, CHUNK)
        return pltpu.make_async_copy(u_s.at[src], u_hbm.at[pl.ds(i * CHUNK, CHUNK)], u_sem.at[i])

    def back(k, carry):
        x = X - 1 - k
        mine, after = carry
        before = u_s[x + 4]
        u_s[x + 5] = GAIN * (mine + after)

        @pl.when(lax.rem(x, CHUNK) == 0)
        def _():
            u_copy(x // CHUNK).start()
        return before, RHO * (after + (mine - RHO * before))

    lax.fori_loop(0, X, back, (u_s[X + 4], jnp.zeros((YT, Z, LANES), F32)))
    mom_ref[0] = u_s[X + 4]
    mom_ref[1] = u_s[5]
    for side, z in ((0, 0), (1, 7)):
        edgepot_ref[side] = pot_s[pl.ds(4 * ROW + z, FACE, stride=Z), :]

    for i in range(NCHUNK):
        pot_copy(i).wait()
        u_copy(i).wait()


def solve_block(flags, act, c, level, xlo, xhi):
    any_spec = pl.BlockSpec(memory_space=pltpu.HBM)
    vm = pl.BlockSpec(memory_space=pltpu.VMEM)
    sm = pl.BlockSpec(memory_space=pltpu.SMEM)
    block = (X, YT, Z, LANES)
    return pl.pallas_call(
        block_kernel,
        in_specs=[sm, sm, any_spec, any_spec, vm, vm],
        out_specs=[any_spec, any_spec, vm, vm],
        out_shape=[
            jax.ShapeDtypeStruct((ROWS, LANES), F32),
            jax.ShapeDtypeStruct(block, F32),
            jax.ShapeDtypeStruct((2, YT, Z, LANES), F32),
            jax.ShapeDtypeStruct((2, FACE, LANES), F32),
        ],
        scratch_shapes=[
            pltpu.VMEM((X + 5, YT, Z, LANES), F32),
            pltpu.VMEM((X + 5, YT, Z, LANES), jnp.int32),
            pltpu.VMEM(((X + 5) * ROW, LANES), F32),
            pltpu.VMEM((X + 5, YT, Z, LANES), F32),
            pltpu.VMEM((7, YT, Z, LANES), F32),
            pltpu.VMEM((2, YT, Z, LANES), F32),
            pltpu.SemaphoreType.DMA((2, NCHUNK)),
            pltpu.SemaphoreType.DMA((NCHUNK,)),
            pltpu.SemaphoreType.DMA((NCHUNK,)),
        ],
        compiler_params=vmem(50),
        cost_estimate=pl.CostEstimate(flops=4 * 10**9, bytes_accessed=60 * 2**20, transcendentals=0),
        name="block",
    )(flags, act, c.reshape(block), level.reshape(block), xlo, xhi)


EXT = X + 2
GROUP = 8


def seam_kernel(flag_ref, pow_ref, own_lo, own_hi, inner_hbm, got_lo, got_hi, xlo_ref, xhi_ref,
                corner_lo_ref, corner_hi_ref, edgepot_hbm, mom_ref, act_ref,
                df_hbm, dpot_hbm, send_ref, ext_s, in_s, df_s, dpot_s, fl_s, acc_s, in_sem, out_sem):
    open_x = (flag_ref[0], flag_ref[1])
    tile_row = lax.broadcasted_iota(jnp.int32, (YT, LANES), 0)
    act = jnp.zeros((YT, LANES), F32)
    for t in range(YT):
        act = jnp.where(tile_row == t, act_ref[t], act)
    shape = (GROUP, YT, LANES)
    open_y = jnp.logical_or(
        lax.broadcasted_iota(jnp.int32, shape, 2) < LANES - 1,
        lax.broadcasted_iota(jnp.int32, shape, 1) < YT - 1,
    )
    row = lax.broadcasted_iota(jnp.int32, shape, 0)
    acc_s[...] = jnp.zeros_like(acc_s)
    main = pl.ds(1, X)

    def arrivals(side):
        own, got = ((own_lo, got_lo), (own_hi, got_hi))[side]
        pairs = [(own.at[0], ext_s.at[side, 0, main]), (own.at[1], ext_s.at[side, 1, main]),
                 (got.at[0], ext_s.at[side, 2, main]), (got.at[1], ext_s.at[side, 3, main]),
                 (got.at[2], in_s.at[side, 0]), (inner_hbm.at[side], in_s.at[side, 1]),
                 (edgepot_hbm.at[side], in_s.at[side, 2])]
        return [pltpu.make_async_copy(far, near, in_sem.at[side, k]) for k, (far, near) in enumerate(pairs)]

    def departures(side):
        at = pl.ds(2 * side, 2)
        return [pltpu.make_async_copy(df_s.at[at], df_hbm.at[at], out_sem.at[side, 0]),
                pltpu.make_async_copy(dpot_s.at[side], dpot_hbm.at[side], out_sem.at[side, 1])]

    for side in range(2):
        for copy in arrivals(side):
            copy.start()

    for side, (corner, z) in enumerate(((corner_lo_ref, 0), (corner_hi_ref, 7))):
        for spot, ref, r, k in ((0, xlo_ref, 1, 0), (EXT - 1, xhi_ref, 0, 1)):
            ext_s[side, 0, spot] = ref[0, r, :, z, :]
            ext_s[side, 1, spot] = half_over_psi(ref[1, r, :, z, :])
            ext_s[side, 2, spot] = corner[2 * k]
            ext_s[side, 3, spot] = half_over_psi(corner[2 * k + 1])

    def one_side(side, _):
        for k in range(2):
            @pl.when(side == k)
            def _():
                for copy in arrivals(k):
                    copy.wait()
        open_z = flag_ref[2 + side]
        bias = 1.0 - open_z
        c0_s, h0_s, cm_s, hm_s, dp_s = (ext_s.at[side, k] for k in range(5))
        got2_s, inner_s, pot_s = (in_s.at[side, k] for k in range(3))

        def first(i, _):
            at = pl.ds(i * 6, 6)
            h0 = h0_s[at]
            flux = recip(h0 + hm_s[at]) * open_z * (cm_s[at] - c0_s[at])
            fl_s[at] = flux
            dp_s[at] = -h0 * flux
            return 0

        lax.fori_loop(0, EXT // 6, first, 0)

        def second(i, _):
            at = pl.ds(i * GROUP, GROUP)
            ext = pl.ds(i * GROUP + 1, GROUP)
            after = pl.ds(i * GROUP + 2, GROUP)
            lo_gate = jnp.where(row == 0, jnp.where(i == 0, open_x[0], 1.0), 1.0)
            hi_gate = jnp.where(row == GROUP - 1, jnp.where(i == X // GROUP - 1, open_x[1], 1.0), 1.0)

            def plane(h_ref, v_ref, extra):
                h, v = h_ref[ext] + extra, v_ref[ext]
                wy = jnp.where(open_y, recip(h + next_y(h)), 0.0)
                fy = wy * (next_y(v) - v)
                total = recip(h + h_ref[at]) * lo_gate * (v_ref[at] - v)
                total = total + recip(h + h_ref[after]) * hi_gate * (v_ref[after] - v)
                return h, v, total + (fy - prev_y(fy))

            hm, cm, across_m = plane(hm_s, cm_s, bias)
            h0, dp, across_0 = plane(h0_s, dp_s, 0.0)
            flux = fl_s[ext]
            potm = cm * (cm * cm - 1.0) - hm * (across_m + got2_s[at] - flux)
            pot0 = pot_s[at] + dp
            h1 = inner_s[at]
            toward = recip(h0 + h1) * dp
            join = recip(h0 + hm) * open_z * (potm - pot0)
            df0 = act * (h0 * (across_0 - toward + join))
            df1 = act * (h1 * toward)
            outer, inner = 3 * side, 1 + side
            df_s[outer, at] = df0
            df_s[inner, at] = df1
            dpot_s[side, at] = dp
            for spot, value in ((outer, df0), (inner, df1)):
                last, start = acc_s[spot], acc_s[4 + spot]
                for r in range(GROUP):
                    x = i * GROUP + r
                    last = last + pow_ref[1, X - 1 - x] * value[r]
                    start = start + pow_ref[1, x] * value[r]
                acc_s[spot] = last
                acc_s[4 + spot] = start
            return 0

        lax.fori_loop(0, X // GROUP, second, 0)
        for copy in departures(side):
            copy.start()
        return 0

    lax.fori_loop(0, 2, one_side, 0)

    sub = sub_iota((Z, LANES))
    half = sub < 4
    for t in range(YT):
        totals = []
        for which in range(2):
            total = mom_ref[which, t]
            for k, z in enumerate((0, 1, 6, 7)):
                line = jnp.broadcast_to(acc_s[4 * which + k, t:t + 1, :], (Z, LANES))
                total = total + jnp.where(sub == z, line, 0.0)
            totals.append(total)
        last, start = totals
        send_ref[2 * t] = jnp.where(half, last, pltpu.roll(start, 4, 0))
        send_ref[2 * t + 1] = jnp.where(half, pltpu.roll(last, 4, 0), start)
    for side in range(2):
        for copy in departures(side):
            copy.wait()


def add_seams(flags, powers, own_lo, own_hi, inner, got_lo, got_hi, xlo, xhi, corner_lo, corner_hi, edgepot, mom, act):
    vm = pl.BlockSpec(memory_space=pltpu.VMEM)
    sm = pl.BlockSpec(memory_space=pltpu.SMEM)
    hbm = pl.BlockSpec(memory_space=pltpu.HBM)
    lines = [a.reshape(a.shape[0], X, YT, LANES) for a in (own_lo, own_hi, inner, got_lo, got_hi)]
    return pl.pallas_call(
        seam_kernel,
        in_specs=[sm, sm] + [hbm] * 5 + [vm] * 4 + [hbm, vm, sm],
        out_specs=[hbm, hbm, vm],
        out_shape=[
            jax.ShapeDtypeStruct((4, X, YT, LANES), F32),
            jax.ShapeDtypeStruct((2, X, YT, LANES), F32),
            jax.ShapeDtypeStruct((32, Z, LANES), F32),
        ],
        scratch_shapes=[
            pltpu.VMEM((2, 5, EXT, YT, LANES), F32),
            pltpu.VMEM((2, 3, X, YT, LANES), F32),
            pltpu.VMEM((4, X, YT, LANES), F32),
            pltpu.VMEM((2, X, YT, LANES), F32),
            pltpu.VMEM((EXT, YT, LANES), F32),
            pltpu.VMEM((8, YT, LANES), F32),
            pltpu.SemaphoreType.DMA((2, 7)),
            pltpu.SemaphoreType.DMA((2, 2)),
        ],
        compiler_params=vmem(50),
        cost_estimate=pl.CostEstimate(flops=10**7, bytes_accessed=12 * 2**20, transcendentals=0),
        name="seams",
    )(flags, powers, *lines, xlo, xhi, corner_lo, corner_hi, edgepot.reshape(2, X, YT, LANES), mom, act)


def lines_kernel(u_hbm, df_hbm, thigh_ref, tlow_ref, edge_ref, out_hbm, u_s, df_s, p_s, w_s, v_s, df_sem, in_sem, out_sem):
    groups = X // MROWS
    grow = MROWS * ROW

    def moves(i):
        at = pl.ds(i * MROWS, MROWS)
        return (pltpu.make_async_copy(u_hbm.at[pl.ds(i * grow, grow)], u_s.at[pl.ds(i * grow, grow)], in_sem.at[i]),
                pltpu.make_async_copy(v_s.at[at], out_hbm.at[at], out_sem.at[i]))

    bring = pltpu.make_async_copy(df_hbm, df_s, df_sem)
    bring.start()
    for i in range(groups):
        moves(i)[0].start()
    bring.wait()
    shape = (4, YT, LANES)

    def forth(x, carry):
        carry = RHO * carry + df_s[:, x]
        p_s[:, x] = carry
        return carry

    lax.fori_loop(0, X, forth, jnp.zeros(shape, F32), unroll=4)

    def back(k, carry):
        x = X - 1 - k
        f = df_s[:, x]
        df_s[:, x] = GAIN * (p_s[:, x] + carry)
        return RHO * (carry + f)

    lax.fori_loop(0, X, back, jnp.zeros(shape, F32), unroll=4)
    edge = edge_ref[...]

    def group(i, _):
        come, leave = moves(i)
        come.wait()
        for n, z in enumerate((0, 1, 6, 7)):
            at = pl.ds(i * grow + z, MROWS * YT, stride=Z)
            added = df_s[n, pl.ds(i * MROWS, MROWS)].reshape(MROWS * YT, LANES)
            u_s[at, :] = u_s[at, :] + added
        table = (thigh_ref[...], tlow_ref[...])
        for b in range(YT // 2):
            pair = [
                jnp.concatenate([
                    u_s[pl.ds(pl.multiple_of(i * grow + x * ROW + (2 * b + k) * Z, Z), Z), :] for x in range(MROWS)
                ], axis=0)
                for k in range(2)
            ]
            solved = dot3(split(jnp.concatenate(pair, axis=1)), table)
            for k in range(2):
                w_s[:, 2 * b + k] = solved[:, k * LANES:(k + 1) * LANES].reshape(MROWS, Z, LANES)

        def body(x, _):
            for t, part in enumerate(y_carry([w_s[x, t] for t in range(YT)], edge)):
                v_s[i * MROWS + x, t] = part
            return 0

        lax.fori_loop(0, MROWS, body, 0, unroll=UNROLL)
        leave.start()
        return 0

    lax.fori_loop(0, groups, group, 0)
    for i in range(groups):
        moves(i)[1].wait()


UNROLL = 16


def solve_lines(u, df, tables):
    vm = pl.BlockSpec(memory_space=pltpu.VMEM)
    hbm = pl.BlockSpec(memory_space=pltpu.HBM)
    block = (X, YT, Z, LANES)
    return pl.pallas_call(
        lines_kernel,
        in_specs=[hbm, hbm] + [vm] * 3,
        out_specs=hbm,
        out_shape=jax.ShapeDtypeStruct(block, F32),
        scratch_shapes=[
            pltpu.VMEM((ROWS, LANES), F32),
            pltpu.VMEM((4, X, YT, LANES), F32),
            pltpu.VMEM((4, X, YT, LANES), F32),
            pltpu.VMEM((MROWS, YT, Z, LANES), F32),
            pltpu.VMEM(block, F32),
            pltpu.SemaphoreType.DMA,
            pltpu.SemaphoreType.DMA((X // MROWS,)),
            pltpu.SemaphoreType.DMA((X // MROWS,)),
        ],
        compiler_params=vmem(50),
        cost_estimate=pl.CostEstimate(flops=2 * 10**9, bytes_accessed=10 * 2**20, transcendentals=0),
        name="lines",
    )(u.reshape(ROWS, LANES), df, *tables)


def mend_kernel(pot_hbm, dpot_hbm, out_hbm, pot_s, dpot_s, in_sem, out_sem):
    def moves(i):
        at, part = pl.ds(i * CHUNK * ROW, CHUNK * ROW), pl.ds(i * PART, PART)
        return (pltpu.make_async_copy(pot_hbm.at[at], pot_s.at[at], in_sem.at[0, i]),
                pltpu.make_async_copy(dpot_hbm.at[:, part], dpot_s.at[:, part], in_sem.at[1, i]),
                pltpu.make_async_copy(pot_s.at[at], out_hbm.at[at], out_sem.at[i]))

    for i in range(NCHUNK):
        moves(i)[0].start()
        moves(i)[1].start()

    def chunk(i, _):
        pot_in, dpot_in, leave = moves(i)
        pot_in.wait()
        dpot_in.wait()
        for side, z in ((0, 0), (1, 7)):
            at = pl.ds(i * CHUNK * ROW + z, PART, stride=Z)
            pot_s[at, :] = pot_s[at, :] + dpot_s[side, pl.ds(i * PART, PART), :]
        leave.start()
        return 0

    lax.fori_loop(0, NCHUNK, chunk, 0)
    for i in range(NCHUNK):
        moves(i)[2].wait()


def mend_potential(pot, dpot):
    hbm = pl.BlockSpec(memory_space=pltpu.HBM)
    return pl.pallas_call(
        mend_kernel,
        in_specs=[hbm, hbm],
        out_specs=hbm,
        out_shape=jax.ShapeDtypeStruct((ROWS, LANES), F32),
        scratch_shapes=[
            pltpu.VMEM((ROWS, LANES), F32),
            pltpu.VMEM((2, FACE, LANES), F32),
            pltpu.SemaphoreType.DMA((2, NCHUNK)),
            pltpu.SemaphoreType.DMA((NCHUNK,)),
        ],
        compiler_params=vmem(50),
        cost_estimate=pl.CostEstimate(flops=10**7, bytes_accessed=10 * 2**20, transcendentals=0),
        name="mend",
    )(pot, dpot.reshape(2, FACE, LANES))


def carries_kernel(count, in_ref, out_ref):
    got = [in_ref[d] for d in range(count)]
    half = sub_iota((8, TILE)) < 4
    hop = rho(X)
    right = [jnp.zeros((8, TILE), F32)]
    for d in range(count - 1):
        right.append(hop * right[-1] + got[d])
    starts = [pltpu.roll(g, 4, 0) for g in got]
    left = [jnp.zeros((8, TILE), F32)]
    for d in range(count - 1, 0, -1):
        left.append(hop * left[-1] + starts[d])
    left = left[::-1]
    from_low, from_high = ends(starts[0] + hop * left[0], got[-1] + hop * right[-1], X * count)
    for d in range(count):
        carry_r = right[d] + rho(X * d) * from_low
        carry_l = left[d] + rho(X * (count - 1 - d)) * from_high
        out_ref[d] = jnp.where(half, carry_r, pltpu.roll(carry_l, 4, 0))


def scan_carries(got):
    vm = pl.BlockSpec(memory_space=pltpu.VMEM)
    return pl.pallas_call(
        functools.partial(carries_kernel, got.shape[0]),
        in_specs=[vm],
        out_specs=vm,
        out_shape=jax.ShapeDtypeStruct(got.shape, F32),
        cost_estimate=pl.CostEstimate(flops=10**6, bytes_accessed=2**18, transcendentals=0),
        name="carries",
    )(got)


FIN = 8


def final_kernel(pow_ref, got_ref, thigh_ref, tlow_ref, edge_ref, v_hbm, out_hbm, v_s, lr_s, in_sem, out_sem):
    def moves(i):
        at = pl.ds(i * FIN * ROW, FIN * ROW)
        return (pltpu.make_async_copy(v_hbm.at[at], v_s.at[at], in_sem.at[i]),
                pltpu.make_async_copy(v_s.at[at], out_hbm.at[at], out_sem.at[i]))

    for i in range(X // FIN):
        moves(i)[0].start()
    half = sub_iota((Z, LANES)) < 4
    edge = edge_ref[...]

    def solve(b, _):
        pair = []
        for k in range(2):
            even, odd = got_ref[4 * b + 2 * k], got_ref[4 * b + 2 * k + 1]
            pair.append(jnp.concatenate([
                jnp.where(half, even, pltpu.roll(odd, 4, 0)),
                jnp.where(half, pltpu.roll(even, 4, 0), odd),
            ], axis=0))
        solved = dot3(split(jnp.concatenate(pair, axis=1)), (thigh_ref[...], tlow_ref[...]))
        for side in range(2):
            for k in range(2):
                lr_s[side, 2 * b + k] = solved[8 * side:8 * side + 8, k * LANES:(k + 1) * LANES]
        return 0

    lax.fori_loop(0, YT // 2, solve, 0)

    def carry(side, _):
        for t, part in enumerate(y_carry([lr_s[side, t] for t in range(YT)], edge)):
            lr_s[side, t] = part
        return 0

    lax.fori_loop(0, 2, carry, 0)

    def chunk(i, _):
        come, leave = moves(i)
        come.wait()

        def row(r, _):
            x = i * FIN + r
            at = pl.ds(pl.multiple_of(x * ROW, ROW), ROW)
            low, high = (lr_s[side].reshape(ROW, LANES) for side in range(2))
            v_s[at, :] = v_s[at, :] + pow_ref[0, x] * low + pow_ref[0, X - 1 - x] * high
            return 0

        lax.fori_loop(0, FIN, row, 0, unroll=2)
        leave.start()
        return 0

    lax.fori_loop(0, X // FIN, chunk, 0)
    for i in range(X // FIN):
        moves(i)[1].wait()


def finish(powers, got, tables, v):
    vm = pl.BlockSpec(memory_space=pltpu.VMEM)
    hbm = pl.BlockSpec(memory_space=pltpu.HBM)
    return pl.pallas_call(
        final_kernel,
        in_specs=[pl.BlockSpec(memory_space=pltpu.SMEM)] + [vm] * 4 + [hbm],
        out_specs=hbm,
        out_shape=jax.ShapeDtypeStruct((ROWS, LANES), F32),
        scratch_shapes=[
            pltpu.VMEM((ROWS, LANES), F32),
            pltpu.VMEM((2, YT, Z, LANES), F32),
            pltpu.SemaphoreType.DMA((X // FIN,)),
            pltpu.SemaphoreType.DMA((X // FIN,)),
        ],
        compiler_params=vmem(50),
        cost_estimate=pl.CostEstimate(flops=10**7, bytes_accessed=10 * 2**20, transcendentals=0),
        name="finish",
    )(powers, got, *tables, v)


def shift(value, axis, forward):
    count = lax.axis_size(axis)
    pairs = [(i, i + 1) for i in range(count - 1)]
    if not forward:
        pairs = [(b, a) for a, b in pairs]
    return lax.ppermute(value, axis, pairs)


def to_tiles(block):
    return block.reshape(X, Z, YT, LANES).transpose(0, 2, 1, 3).reshape(ROWS, LANES)


def from_tiles(rows):
    return rows.reshape(X, YT, Z, LANES).transpose(0, 2, 1, 3).reshape(X, Z, Y)


def per_device(concentration, psi_level, tile_mask):
    c, level = to_tiles(concentration), to_tiles(psi_level)
    xy, gz = lax.axis_index("xy"), lax.axis_index("gz")
    n_xy, n_gz = lax.axis_size("xy"), lax.axis_size("gz")
    flags = jnp.stack([xy > 0, xy < n_xy - 1, gz > 0, gz < n_gz - 1]).astype(F32)
    mask_row = lax.dynamic_index_in_dim(tile_mask, xy * X // TILE, 0, keepdims=False)
    act = mask_row.astype(F32) * (2.0 * TIME_STEP)
    tables = tuple(jnp.asarray(t) for t in y_tables())
    steps = np.exp(-THETA * np.arange(X + 1))
    powers = jnp.asarray(np.stack([steps[1:], GAIN * steps[:-1]]).astype(np.float32))

    zlo, zhi, inner, xlo, xhi = make_faces(c, level)
    pair = (2, 2, YT, Z, LANES)
    got_xlo = shift(xhi, "xy", True).reshape(pair)
    got_xhi = shift(xlo, "xy", False).reshape(pair)
    got_zlo = shift(zhi, "gz", True)
    got_zhi = shift(zlo, "gz", False)

    def corners(z):
        return jnp.stack([got_xlo[0, 1, :, z], got_xlo[1, 1, :, z], got_xhi[0, 0, :, z], got_xhi[1, 0, :, z]])

    corner_lo = shift(corners(7), "gz", True)
    corner_hi = shift(corners(0), "gz", False)

    pot, u, mom, edgepot = solve_block(flags, act, c, level, got_xlo, got_xhi)
    df, dpot, send = add_seams(
        flags, powers, zlo, zhi, inner, got_zlo, got_zhi, got_xlo, got_xhi, corner_lo, corner_hi, edgepot, mom, act,
    )
    got = lax.all_to_all(send, "xy", split_axis=0, concat_axis=0, tiled=True)
    v = solve_lines(u, df, tables)
    got, v = lax.optimization_barrier((got, v))
    carried, pot = lax.optimization_barrier((scan_carries(got), pot))
    back = lax.all_to_all(carried, "xy", split_axis=0, concat_axis=0, tiled=True)
    potential = mend_potential(pot, dpot)
    increment = finish(powers, back, tables, v.reshape(ROWS, LANES))
    return from_tiles(potential), from_tiles(increment)


def solution(mesh):
    placed = (P("xy", "gz", None), P("xy", "gz", None), P())
    return jax.shard_map(
        per_device,
        mesh=mesh,
        in_specs=placed,
        out_specs=(P("xy", "gz", None), P("xy", "gz", None)),
        check_vma=False,
    )
```

```python
import functools
import math

import jax
import jax.numpy as jnp
import numpy as np
from jax import lax
from jax.experimental import pallas as pl
from jax.experimental.pallas import tpu as pltpu
from jax.sharding import PartitionSpec as P

TILE = 128
LEVELS = 4096
STIFF = 4096
GRADIENT_COEF = 0.5
TIME_STEP = 32.0
PSI_FLOOR = 0.25

X = 64
Z = 8
Y = 2048
YT = 16
LANES = 128
ROW = YT * Z
ROWS = X * ROW
FACE = X * YT
LINE = 2048
NB = 256
F32 = jnp.float32
BF16 = jnp.bfloat16

_half = 1.0 + 0.5 / STIFF
THETA = math.log(_half + math.sqrt(_half * _half - 1.0))
RHO = math.exp(-THETA)
GAIN = (RHO / STIFF) / (1.0 - RHO * RHO)


def rho(power):
    return math.exp(-THETA * power)


def vmem(limit_mib):
    return pltpu.CompilerParams(vmem_limit_bytes=limit_mib * 2**20)


def half_over_psi(level):
    return recip(2.0 * PSI_FLOOR + level.astype(F32) * (2.0 * (1.0 - PSI_FLOOR) / (LEVELS - 1)))


def recip(value):
    return pl.reciprocal(value, approx=True)


def lane_iota(shape):
    return lax.broadcasted_iota(jnp.int32, shape, len(shape) - 1)


def sub_iota(shape):
    return lax.broadcasted_iota(jnp.int32, shape, len(shape) - 2)


def next_y(v):
    axis = v.ndim - 1
    turned = pltpu.roll(v, LANES - 1, axis)
    if TILES_LEAD[v.shape[-2]]:
        following = jnp.concatenate([turned[1:], turned[:1]], axis=0)
    else:
        following = pltpu.roll(turned, YT - 1, axis - 1)
    return jnp.where(lane_iota(v.shape) == LANES - 1, following, turned)


def prev_y(v):
    axis = v.ndim - 1
    turned = pltpu.roll(v, 1, axis)
    if TILES_LEAD[v.shape[-2]]:
        previous = jnp.concatenate([turned[-1:], turned[:-1]], axis=0)
    else:
        previous = pltpu.roll(turned, 1, axis - 1)
    return jnp.where(lane_iota(v.shape) == 0, previous, turned)


TILES_LEAD = {Z: True, YT: False}


def next_z(v):
    return pltpu.roll(v, Z - 1, 1)


def prev_z(v):
    return pltpu.roll(v, 1, 1)


CHUNK = 8
NCHUNK = X // CHUNK
PART = CHUNK * YT


def faces_kernel(c_hbm, l_hbm, zlo_hbm, zhi_hbm, in_hbm, xlo_ref, xhi_ref, c_s, l_s, z_s, i_s, in_sem, out_sem):
    def arrivals(i):
        at = pl.ds(i * CHUNK * ROW, CHUNK * ROW)
        return (pltpu.make_async_copy(c_hbm.at[at], c_s.at[at], in_sem.at[0, i]),
                pltpu.make_async_copy(l_hbm.at[at], l_s.at[at], in_sem.at[1, i]))

    def departures(i):
        at = pl.ds(i * PART, PART)
        pairs = ((z_s.at[0, :, at], zlo_hbm.at[:, at]), (z_s.at[1, :, at], zhi_hbm.at[:, at]),
                 (i_s.at[:, at], in_hbm.at[:, at]))
        return [pltpu.make_async_copy(near, far, out_sem.at[k, i]) for k, (near, far) in enumerate(pairs)]

    for i in range(NCHUNK):
        for copy in arrivals(i):
            copy.start()

    def chunk(i, _):
        for copy in arrivals(i):
            copy.wait()
        out = pl.ds(i * PART, PART)

        def plane(ref, z):
            return ref[pl.ds(i * CHUNK * ROW + z, PART, stride=Z), :]

        for side, edge, inner in ((0, 0, 1), (1, 7, 6)):
            c_edge, c_inner = plane(c_s, edge), plane(c_s, inner)
            h_edge = half_over_psi(plane(l_s, edge))
            h_inner = half_over_psi(plane(l_s, inner))
            z_s[side, 0, out] = c_edge
            z_s[side, 1, out] = h_edge
            z_s[side, 2, out] = recip(h_edge + h_inner) * (c_inner - c_edge)
            i_s[side, out] = h_inner
        for copy in departures(i):
            copy.start()
        return 0

    lax.fori_loop(0, NCHUNK, chunk, 0)
    last = (X - 2) * ROW
    for ref, at in ((xlo_ref, 0), (xhi_ref, last)):
        ref[0] = c_s[at:at + 2 * ROW, :]
        ref[1] = l_s[at:at + 2 * ROW, :].astype(F32)
    for i in range(NCHUNK):
        for copy in departures(i):
            copy.wait()


def make_faces(c, level):
    hbm = pl.BlockSpec(memory_space=pltpu.HBM)
    vm = pl.BlockSpec(memory_space=pltpu.VMEM)
    return pl.pallas_call(
        faces_kernel,
        in_specs=[hbm, hbm],
        out_specs=[hbm, hbm, hbm, vm, vm],
        out_shape=[
            jax.ShapeDtypeStruct((3, FACE, LANES), F32),
            jax.ShapeDtypeStruct((3, FACE, LANES), F32),
            jax.ShapeDtypeStruct((2, FACE, LANES), F32),
            jax.ShapeDtypeStruct((2, 2 * ROW, LANES), F32),
            jax.ShapeDtypeStruct((2, 2 * ROW, LANES), F32),
        ],
        scratch_shapes=[
            pltpu.VMEM((ROWS, LANES), F32),
            pltpu.VMEM((ROWS, LANES), jnp.int32),
            pltpu.VMEM((2, 3, FACE, LANES), F32),
            pltpu.VMEM((2, FACE, LANES), F32),
            pltpu.SemaphoreType.DMA((2, NCHUNK)),
            pltpu.SemaphoreType.DMA((3, NCHUNK)),
        ],
        compiler_params=vmem(50),
        cost_estimate=pl.CostEstimate(flops=10**6, bytes_accessed=13 * 2**20, transcendentals=0),
        name="faces",
    )(c, level)


def y_tables():
    idx = np.arange(NB)
    table = GAIN * np.exp(-THETA * np.abs(idx[:, None] - idx[None, :]))
    parts, rest = [], table
    for _ in range(3):
        parts.append(rest.astype(jnp.bfloat16))
        rest = rest - parts[-1].astype(np.float64)
    fwd = np.exp(-THETA * (idx + 1.0))
    bwd = np.exp(-THETA * (NB - idx.astype(np.float64)))
    edge = np.zeros((8, LANES), np.float32)
    edge[0], edge[1] = fwd[:LANES], fwd[LANES:]
    edge[2], edge[3] = bwd[:LANES], bwd[LANES:]
    return np.stack(parts), edge


def split(v):
    high = v.astype(BF16)
    rest = v - high.astype(F32)
    middle = rest.astype(BF16)
    return high, middle, (rest - middle.astype(F32)).astype(BF16)


def dot6(value, table_ref):
    terms = split(value)
    rows = value.shape[0]
    total = None
    for k in (2, 1, 0):
        left = jnp.concatenate(terms[:3 - k], axis=0) if k < 2 else terms[0]
        product = jnp.dot(left, table_ref[k], preferred_element_type=F32)
        for i in reversed(range(3 - k)):
            piece = product[i * rows:(i + 1) * rows]
            total = piece if total is None else total + piece
    return total


def ends(first, last, length):
    scale = 1.0 / (1.0 - rho(2 * length))
    tail = rho(length)
    return (first + tail * last) * scale, (last + tail * first) * scale


def y_carry(tiles, edge):
    count = YT // 2
    heads = [jnp.broadcast_to(tiles[2 * b][:, 0:1], (8, LANES)) for b in range(count)]
    tails = [jnp.broadcast_to(tiles[2 * b + 1][:, LANES - 1:LANES], (8, LANES)) for b in range(count)]
    hop = rho(NB)
    right = [jnp.zeros_like(heads[0])]
    for b in range(count - 1):
        right.append(hop * right[-1] + tails[b])
    left = [jnp.zeros_like(heads[0])]
    for b in range(count - 1, 0, -1):
        left.append(hop * left[-1] + heads[b])
    left = left[::-1]
    from_low, from_high = ends(heads[0] + hop * left[0], tails[-1] + hop * right[-1], Y)
    out = []
    for b in range(count):
        carry_r = right[b] + rho(NB * b) * from_low
        carry_l = left[b] + rho(NB * (count - 1 - b)) * from_high
        for k in range(2):
            out.append(tiles[2 * b + k] + carry_r * edge[k:k + 1, :] + carry_l * edge[2 + k:3 + k, :])
    return out


MROWS = 16


def block_kernel(flag_ref, act_ref, c_hbm, l_hbm, xlo_ref, xhi_ref,
                 pot_hbm, u_hbm, mom_ref, edgepot_ref,
                 c_s, l_s, pot_s, u_s, st, in_sem, pot_sem, u_sem):
    def copies_in(i):
        at = pl.ds(i * CHUNK, CHUNK)
        return (pltpu.make_async_copy(c_hbm.at[at], c_s.at[pl.ds(i * CHUNK + 3, CHUNK)], in_sem.at[0, i]),
                pltpu.make_async_copy(l_hbm.at[at], l_s.at[pl.ds(i * CHUNK + 3, CHUNK)], in_sem.at[1, i]))

    for i in range(NCHUNK):
        for copy in copies_in(i):
            copy.start()

    tile = (Z, LANES)
    sub, lane = sub_iota(tile), lane_iota(tile)
    top, first, last = sub == Z - 1, lane == 0, lane == LANES - 1
    WZ, WY, WX, BASE, REST, POT, SWEEP, H1, H2 = range(9)

    def up_z(v):
        return pltpu.roll(v, Z - 1, 0)

    def down_z(v):
        return pltpu.roll(v, 1, 0)

    def up_y(v):
        return pltpu.roll(v, LANES - 1, 1)

    def down_y(v):
        return pltpu.roll(v, 1, 1)

    def ptile(e, t):
        return pl.ds(pl.multiple_of(e * ROW + t * Z, Z), Z)

    def advance(e, load, store):
        open_x = jnp.where(e <= 3, open_lo, jnp.where(e >= X + 3, open_hi, 1.0))
        inside = jnp.where(e >= 5, 1.0, 0.0)
        h = half_over_psi(l_s[e, 0])
        up_h, up_c = up_y(h), up_y(c_s[e, 0])
        below = below2 = jnp.zeros(tile, F32)
        held = None

        def second(t, pot1, up_pot, gx2, wz, wy, up_next, below2):
            gz = wz * (up_z(pot1) - pot1)
            gy = wy * (jnp.where(last, up_next, up_pot) - pot1)
            turned = down_y(gy)
            store(REST, t, (gz - down_z(gz)) + (gy - jnp.where(first, below2, turned)) - gx2)
            return turned

        for t in range(YT):
            c = c_s[e, t]
            if t + 1 < YT:
                h_next = half_over_psi(l_s[e, t + 1])
                up_h_next, up_c_next = up_y(h_next), up_y(c_s[e, t + 1])
            else:
                h_next, up_h_next, up_c_next = h, up_h, up_c
            h1 = load(H1, t)
            wx = recip(h1 + h) * open_x
            fx = wx * (c - c_s[e - 1, t])
            pot1 = load(BASE, t) - h1 * fx
            gx2 = load(WX, t) * (pot1 - load(POT, t))
            rhs = (act_ref[t] * inside) * (load(H2, t) * (load(REST, t) + gx2))
            swept = RHO * load(SWEEP, t) + rhs
            u_s[e, t] = swept
            pot_s[ptile(e, t), :] = pot1
            wz_old, wy_old = load(WZ, t), load(WY, t)
            wz = jnp.where(top, 0.0, recip(h + up_z(h)))
            wy = recip(h + jnp.where(last, up_h_next, up_h))
            if t == YT - 1:
                wy = jnp.where(last, 0.0, wy)
            fz = wz * (up_z(c) - c)
            fy = wy * (jnp.where(last, up_c_next, up_c) - c)
            turned = down_y(fy)
            total = (fz - down_z(fz)) + (fy - jnp.where(first, below, turned)) - fx
            below = turned
            for kind, value in ((SWEEP, swept), (POT, pot1), (BASE, c * (c * c - 1.0) - h * total),
                                (WZ, wz), (WY, wy), (WX, wx), (H1, h), (H2, h1)):
                store(kind, t, value)
            up_pot = up_y(pot1)
            if held is not None:
                below2 = second(*held, up_pot, below2)
            held = (t, pot1, up_pot, gx2, wz_old, wy_old)
            h, up_h, up_c = h_next, up_h_next, up_c_next
            yield
        second(*held, held[2], below2)
        yield

    def two_rows(e):
        between = {}

        def keep(kind, t, value):
            between[kind, t] = value

        def put(kind, t, value):
            st[kind, t] = value

        ahead = advance(e, lambda kind, t: st[kind, t], keep)
        behind = advance(e + 1, lambda kind, t: between.pop((kind, t)), put)
        next(ahead)
        for _ in range(YT):
            next(ahead)
            next(behind)
        next(behind)

    open_lo, open_hi = flag_ref[0], flag_ref[1]
    st[...] = jnp.zeros_like(st)
    st[H1:] = jnp.ones((2, YT, Z, LANES), F32)
    c_s[0] = jnp.zeros((YT, Z, LANES), F32)
    for at, ref in ((1, xlo_ref), (X + 3, xhi_ref)):
        c_s[at:at + 2] = ref[0]
        l_s[at:at + 2] = ref[1].astype(jnp.int32)

    def pot_copy(i):
        src = pl.ds((i * CHUNK + 4) * ROW, CHUNK * ROW)
        return pltpu.make_async_copy(pot_s.at[src], pot_hbm.at[pl.ds(i * CHUNK * ROW, CHUNK * ROW)], pot_sem.at[i])

    pairs = CHUNK // 2

    def rows(j, _):
        turn = lax.rem(j, pairs) == 1

        @pl.when(jnp.logical_and(turn, j < X // 2))
        def _():
            for copy in copies_in((j - 1) // pairs):
                copy.wait()

        two_rows(2 * j + 1)

        @pl.when(jnp.logical_and(turn, j > pairs))
        def _():
            pot_copy((j - 1) // pairs - 1).start()
        return 0

    lax.fori_loop(0, X // 2 + 2, rows, 0)

    def u_copy(i):
        src = pl.ds(i * CHUNK + 5, CHUNK)
        return pltpu.make_async_copy(u_s.at[src], u_hbm.at[pl.ds(i * CHUNK, CHUNK)], u_sem.at[i])

    def back(k, carry):
        x = X - 1 - k
        mine, after = carry
        before = u_s[x + 4]
        u_s[x + 5] = GAIN * (mine + after)

        @pl.when(lax.rem(x, CHUNK) == 0)
        def _():
            u_copy(x // CHUNK).start()
        return before, RHO * (after + (mine - RHO * before))

    lax.fori_loop(0, X, back, (u_s[X + 4], jnp.zeros((YT, Z, LANES), F32)))
    mom_ref[0] = u_s[X + 4]
    mom_ref[1] = u_s[5]
    for side, z in ((0, 0), (1, 7)):
        edgepot_ref[side] = pot_s[pl.ds(4 * ROW + z, FACE, stride=Z), :]

    for i in range(NCHUNK):
        pot_copy(i).wait()
        u_copy(i).wait()


def solve_block(flags, act, c, level, xlo, xhi):
    any_spec = pl.BlockSpec(memory_space=pltpu.HBM)
    vm = pl.BlockSpec(memory_space=pltpu.VMEM)
    sm = pl.BlockSpec(memory_space=pltpu.SMEM)
    block = (X, YT, Z, LANES)
    return pl.pallas_call(
        block_kernel,
        in_specs=[sm, sm, any_spec, any_spec, vm, vm],
        out_specs=[any_spec, any_spec, vm, vm],
        out_shape=[
            jax.ShapeDtypeStruct((ROWS, LANES), F32),
            jax.ShapeDtypeStruct(block, F32),
            jax.ShapeDtypeStruct((2, YT, Z, LANES), F32),
            jax.ShapeDtypeStruct((2, FACE, LANES), F32),
        ],
        scratch_shapes=[
            pltpu.VMEM((X + 5, YT, Z, LANES), F32),
            pltpu.VMEM((X + 5, YT, Z, LANES), jnp.int32),
            pltpu.VMEM(((X + 5) * ROW, LANES), F32),
            pltpu.VMEM((X + 5, YT, Z, LANES), F32),
            pltpu.VMEM((9, YT, Z, LANES), F32),
            pltpu.SemaphoreType.DMA((2, NCHUNK)),
            pltpu.SemaphoreType.DMA((NCHUNK,)),
            pltpu.SemaphoreType.DMA((NCHUNK,)),
        ],
        compiler_params=vmem(50),
        cost_estimate=pl.CostEstimate(flops=4 * 10**9, bytes_accessed=60 * 2**20, transcendentals=0),
        name="block",
    )(flags, act, c.reshape(block), level.reshape(block), xlo, xhi)


EXT = X + 2
GROUP = 8


def seam_kernel(flag_ref, pow_ref, own_lo, own_hi, inner_hbm, got_lo, got_hi, xlo_ref, xhi_ref,
                corner_lo_ref, corner_hi_ref, edgepot_hbm, mom_ref, act_ref,
                df_hbm, dpot_hbm, send_ref, ext_s, in_s, df_s, dpot_s, fl_s, acc_s, in_sem, out_sem):
    open_x = (flag_ref[0], flag_ref[1])
    tile_row = lax.broadcasted_iota(jnp.int32, (YT, LANES), 0)
    act = jnp.zeros((YT, LANES), F32)
    for t in range(YT):
        act = jnp.where(tile_row == t, act_ref[t], act)
    shape = (GROUP, YT, LANES)
    open_y = jnp.logical_or(
        lax.broadcasted_iota(jnp.int32, shape, 2) < LANES - 1,
        lax.broadcasted_iota(jnp.int32, shape, 1) < YT - 1,
    )
    row = lax.broadcasted_iota(jnp.int32, shape, 0)
    acc_s[...] = jnp.zeros_like(acc_s)
    main = pl.ds(1, X)

    def arrivals(side):
        own, got = ((own_lo, got_lo), (own_hi, got_hi))[side]
        pairs = [(own.at[0], ext_s.at[side, 0, main]), (own.at[1], ext_s.at[side, 1, main]),
                 (got.at[0], ext_s.at[side, 2, main]), (got.at[1], ext_s.at[side, 3, main]),
                 (got.at[2], in_s.at[side, 0]), (inner_hbm.at[side], in_s.at[side, 1]),
                 (edgepot_hbm.at[side], in_s.at[side, 2])]
        return [pltpu.make_async_copy(far, near, in_sem.at[side, k]) for k, (far, near) in enumerate(pairs)]

    def departures(side):
        at = pl.ds(2 * side, 2)
        return [pltpu.make_async_copy(df_s.at[at], df_hbm.at[at], out_sem.at[side, 0]),
                pltpu.make_async_copy(dpot_s.at[side], dpot_hbm.at[side], out_sem.at[side, 1])]

    for side in range(2):
        for copy in arrivals(side):
            copy.start()

    for side, (corner, z) in enumerate(((corner_lo_ref, 0), (corner_hi_ref, 7))):
        for spot, ref, r, k in ((0, xlo_ref, 1, 0), (EXT - 1, xhi_ref, 0, 1)):
            ext_s[side, 0, spot] = ref[0, r, :, z, :]
            ext_s[side, 1, spot] = half_over_psi(ref[1, r, :, z, :])
            ext_s[side, 2, spot] = corner[2 * k]
            ext_s[side, 3, spot] = half_over_psi(corner[2 * k + 1])

    def one_side(side, _):
        for k in range(2):
            @pl.when(side == k)
            def _():
                for copy in arrivals(k)[:4]:
                    copy.wait()
        open_z = flag_ref[2 + side]
        bias = 1.0 - open_z
        c0_s, h0_s, cm_s, hm_s, dp_s = (ext_s.at[side, k] for k in range(5))
        got2_s, inner_s, pot_s = (in_s.at[side, k] for k in range(3))

        def first(i, _):
            at = pl.ds(i * 6, 6)
            h0 = h0_s[at]
            flux = recip(h0 + hm_s[at]) * open_z * (cm_s[at] - c0_s[at])
            fl_s[at] = flux
            dp_s[at] = -h0 * flux
            return 0

        lax.fori_loop(0, EXT // 6, first, 0)
        for k in range(2):
            @pl.when(side == k)
            def _():
                for copy in arrivals(k)[4:]:
                    copy.wait()

        def second(i, _):
            at = pl.ds(i * GROUP, GROUP)
            ext = pl.ds(i * GROUP + 1, GROUP)
            after = pl.ds(i * GROUP + 2, GROUP)
            lo_gate = jnp.where(row == 0, jnp.where(i == 0, open_x[0], 1.0), 1.0)
            hi_gate = jnp.where(row == GROUP - 1, jnp.where(i == X // GROUP - 1, open_x[1], 1.0), 1.0)

            def plane(h_ref, v_ref, extra):
                h, v = h_ref[ext] + extra, v_ref[ext]
                wy = jnp.where(open_y, recip(h + next_y(h)), 0.0)
                fy = wy * (next_y(v) - v)
                total = recip(h + h_ref[at]) * lo_gate * (v_ref[at] - v)
                total = total + recip(h + h_ref[after]) * hi_gate * (v_ref[after] - v)
                return h, v, total + (fy - prev_y(fy))

            hm, cm, across_m = plane(hm_s, cm_s, bias)
            h0, dp, across_0 = plane(h0_s, dp_s, 0.0)
            flux = fl_s[ext]
            potm = cm * (cm * cm - 1.0) - hm * (across_m + got2_s[at] - flux)
            pot0 = pot_s[at] + dp
            h1 = inner_s[at]
            toward = recip(h0 + h1) * dp
            join = recip(h0 + hm) * open_z * (potm - pot0)
            df0 = act * (h0 * (across_0 - toward + join))
            df1 = act * (h1 * toward)
            outer, inner = 3 * side, 1 + side
            df_s[outer, at] = df0
            df_s[inner, at] = df1
            dpot_s[side, at] = dp
            for spot, value in ((outer, df0), (inner, df1)):
                last, start = acc_s[spot], acc_s[4 + spot]
                for r in range(GROUP):
                    x = i * GROUP + r
                    last = last + pow_ref[1, X - 1 - x] * value[r]
                    start = start + pow_ref[1, x] * value[r]
                acc_s[spot] = last
                acc_s[4 + spot] = start
            return 0

        lax.fori_loop(0, X // GROUP, second, 0)
        for copy in departures(side):
            copy.start()
        return 0

    lax.fori_loop(0, 2, one_side, 0)

    sub = sub_iota((Z, LANES))
    half = sub < 4
    for t in range(YT):
        totals = []
        for which in range(2):
            total = mom_ref[which, t]
            for k, z in enumerate((0, 1, 6, 7)):
                line = jnp.broadcast_to(acc_s[4 * which + k, t:t + 1, :], (Z, LANES))
                total = total + jnp.where(sub == z, line, 0.0)
            totals.append(total)
        last, start = totals
        send_ref[2 * t] = jnp.where(half, last, pltpu.roll(start, 4, 0))
        send_ref[2 * t + 1] = jnp.where(half, pltpu.roll(last, 4, 0), start)
    for side in range(2):
        for copy in departures(side):
            copy.wait()


def add_seams(flags, powers, own_lo, own_hi, inner, got_lo, got_hi, xlo, xhi, corner_lo, corner_hi, edgepot, mom, act):
    vm = pl.BlockSpec(memory_space=pltpu.VMEM)
    sm = pl.BlockSpec(memory_space=pltpu.SMEM)
    hbm = pl.BlockSpec(memory_space=pltpu.HBM)
    lines = [a.reshape(a.shape[0], X, YT, LANES) for a in (own_lo, own_hi, inner, got_lo, got_hi)]
    return pl.pallas_call(
        seam_kernel,
        in_specs=[sm, sm] + [hbm] * 5 + [vm] * 4 + [hbm, vm, sm],
        out_specs=[hbm, hbm, vm],
        out_shape=[
            jax.ShapeDtypeStruct((4, X, YT, LANES), F32),
            jax.ShapeDtypeStruct((2, X, YT, LANES), F32),
            jax.ShapeDtypeStruct((32, Z, LANES), F32),
        ],
        scratch_shapes=[
            pltpu.VMEM((2, 5, EXT, YT, LANES), F32),
            pltpu.VMEM((2, 3, X, YT, LANES), F32),
            pltpu.VMEM((4, X, YT, LANES), F32),
            pltpu.VMEM((2, X, YT, LANES), F32),
            pltpu.VMEM((EXT, YT, LANES), F32),
            pltpu.VMEM((8, YT, LANES), F32),
            pltpu.SemaphoreType.DMA((2, 7)),
            pltpu.SemaphoreType.DMA((2, 2)),
        ],
        compiler_params=vmem(50),
        cost_estimate=pl.CostEstimate(flops=10**7, bytes_accessed=12 * 2**20, transcendentals=0),
        name="seams",
    )(flags, powers, *lines, xlo, xhi, corner_lo, corner_hi, edgepot.reshape(2, X, YT, LANES), mom, act)


def lines_kernel(u_hbm, df_hbm, table_ref, edge_ref, out_hbm, u_s, df_s, p_s, w_s, v_s, df_sem, in_sem, out_sem):
    groups = X // MROWS
    grow = MROWS * ROW

    def moves(i):
        at = pl.ds(i * MROWS, MROWS)
        return (pltpu.make_async_copy(u_hbm.at[pl.ds(i * grow, grow)], u_s.at[pl.ds(i * grow, grow)], in_sem.at[i]),
                pltpu.make_async_copy(v_s.at[at], out_hbm.at[at], out_sem.at[i]))

    bring = pltpu.make_async_copy(df_hbm, df_s, df_sem)
    bring.start()
    for i in range(groups):
        moves(i)[0].start()
    bring.wait()
    shape = (4, YT, LANES)

    def forth(x, carry):
        carry = RHO * carry + df_s[:, x]
        p_s[:, x] = carry
        return carry

    lax.fori_loop(0, X, forth, jnp.zeros(shape, F32), unroll=4)

    def back(k, carry):
        x = X - 1 - k
        f = df_s[:, x]
        df_s[:, x] = GAIN * (p_s[:, x] + carry)
        return RHO * (carry + f)

    lax.fori_loop(0, X, back, jnp.zeros(shape, F32), unroll=4)
    edge = edge_ref[...]

    def group(i, _):
        come, leave = moves(i)
        come.wait()
        for n, z in enumerate((0, 1, 6, 7)):
            at = pl.ds(i * grow + z, MROWS * YT, stride=Z)
            added = df_s[n, pl.ds(i * MROWS, MROWS)].reshape(MROWS * YT, LANES)
            u_s[at, :] = u_s[at, :] + added
        for b in range(YT // 2):
            pair = [
                jnp.concatenate([
                    u_s[pl.ds(pl.multiple_of(i * grow + x * ROW + (2 * b + k) * Z, Z), Z), :] for x in range(MROWS)
                ], axis=0)
                for k in range(2)
            ]
            solved = dot6(jnp.concatenate(pair, axis=1), table_ref)
            for k in range(2):
                w_s[:, 2 * b + k] = solved[:, k * LANES:(k + 1) * LANES].reshape(MROWS, Z, LANES)

        def body(x, _):
            for t, part in enumerate(y_carry([w_s[x, t] for t in range(YT)], edge)):
                v_s[i * MROWS + x, t] = part
            return 0

        lax.fori_loop(0, MROWS, body, 0, unroll=UNROLL)
        leave.start()
        return 0

    lax.fori_loop(0, groups, group, 0)
    for i in range(groups):
        moves(i)[1].wait()


UNROLL = 16


def solve_lines(u, df, tables):
    vm = pl.BlockSpec(memory_space=pltpu.VMEM)
    hbm = pl.BlockSpec(memory_space=pltpu.HBM)
    block = (X, YT, Z, LANES)
    return pl.pallas_call(
        lines_kernel,
        in_specs=[hbm, hbm] + [vm] * 2,
        out_specs=hbm,
        out_shape=jax.ShapeDtypeStruct(block, F32),
        scratch_shapes=[
            pltpu.VMEM((ROWS, LANES), F32),
            pltpu.VMEM((4, X, YT, LANES), F32),
            pltpu.VMEM((4, X, YT, LANES), F32),
            pltpu.VMEM((MROWS, YT, Z, LANES), F32),
            pltpu.VMEM(block, F32),
            pltpu.SemaphoreType.DMA,
            pltpu.SemaphoreType.DMA((X // MROWS,)),
            pltpu.SemaphoreType.DMA((X // MROWS,)),
        ],
        compiler_params=vmem(50),
        cost_estimate=pl.CostEstimate(flops=2 * 10**9, bytes_accessed=10 * 2**20, transcendentals=0),
        name="lines",
    )(u.reshape(ROWS, LANES), df, *tables)


def mend_kernel(pot_hbm, dpot_hbm, out_hbm, pot_s, dpot_s, in_sem, out_sem):
    def moves(i):
        at, part = pl.ds(i * CHUNK * ROW, CHUNK * ROW), pl.ds(i * PART, PART)
        return (pltpu.make_async_copy(pot_hbm.at[at], pot_s.at[at], in_sem.at[0, i]),
                pltpu.make_async_copy(dpot_hbm.at[:, part], dpot_s.at[:, part], in_sem.at[1, i]),
                pltpu.make_async_copy(pot_s.at[at], out_hbm.at[at], out_sem.at[i]))

    for i in range(NCHUNK):
        moves(i)[0].start()
        moves(i)[1].start()

    def chunk(i, _):
        pot_in, dpot_in, leave = moves(i)
        pot_in.wait()
        dpot_in.wait()
        for side, z in ((0, 0), (1, 7)):
            at = pl.ds(i * CHUNK * ROW + z, PART, stride=Z)
            pot_s[at, :] = pot_s[at, :] + dpot_s[side, pl.ds(i * PART, PART), :]
        leave.start()
        return 0

    lax.fori_loop(0, NCHUNK, chunk, 0)
    for i in range(NCHUNK):
        moves(i)[2].wait()


def mend_potential(pot, dpot):
    hbm = pl.BlockSpec(memory_space=pltpu.HBM)
    return pl.pallas_call(
        mend_kernel,
        in_specs=[hbm, hbm],
        out_specs=hbm,
        out_shape=jax.ShapeDtypeStruct((ROWS, LANES), F32),
        scratch_shapes=[
            pltpu.VMEM((ROWS, LANES), F32),
            pltpu.VMEM((2, FACE, LANES), F32),
            pltpu.SemaphoreType.DMA((2, NCHUNK)),
            pltpu.SemaphoreType.DMA((NCHUNK,)),
        ],
        compiler_params=vmem(50),
        cost_estimate=pl.CostEstimate(flops=10**7, bytes_accessed=10 * 2**20, transcendentals=0),
        name="mend",
    )(pot, dpot.reshape(2, FACE, LANES))


def carries_kernel(count, in_ref, out_ref):
    got = [in_ref[d] for d in range(count)]
    half = sub_iota((8, TILE)) < 4
    hop = rho(X)
    right = [jnp.zeros((8, TILE), F32)]
    for d in range(count - 1):
        right.append(hop * right[-1] + got[d])
    starts = [pltpu.roll(g, 4, 0) for g in got]
    left = [jnp.zeros((8, TILE), F32)]
    for d in range(count - 1, 0, -1):
        left.append(hop * left[-1] + starts[d])
    left = left[::-1]
    from_low, from_high = ends(starts[0] + hop * left[0], got[-1] + hop * right[-1], X * count)
    for d in range(count):
        carry_r = right[d] + rho(X * d) * from_low
        carry_l = left[d] + rho(X * (count - 1 - d)) * from_high
        out_ref[d] = jnp.where(half, carry_r, pltpu.roll(carry_l, 4, 0))


def scan_carries(got):
    vm = pl.BlockSpec(memory_space=pltpu.VMEM)
    return pl.pallas_call(
        functools.partial(carries_kernel, got.shape[0]),
        in_specs=[vm],
        out_specs=vm,
        out_shape=jax.ShapeDtypeStruct(got.shape, F32),
        cost_estimate=pl.CostEstimate(flops=10**6, bytes_accessed=2**18, transcendentals=0),
        name="carries",
    )(got)


FIN = 8


def final_kernel(pow_ref, got_ref, table_ref, edge_ref, v_hbm, out_hbm, v_s, lr_s, in_sem, out_sem):
    def moves(i):
        at = pl.ds(i * FIN * ROW, FIN * ROW)
        return (pltpu.make_async_copy(v_hbm.at[at], v_s.at[at], in_sem.at[i]),
                pltpu.make_async_copy(v_s.at[at], out_hbm.at[at], out_sem.at[i]))

    for i in range(X // FIN):
        moves(i)[0].start()
    half = sub_iota((Z, LANES)) < 4
    edge = edge_ref[...]

    def solve(b, _):
        pair = []
        for k in range(2):
            even, odd = got_ref[4 * b + 2 * k], got_ref[4 * b + 2 * k + 1]
            pair.append(jnp.concatenate([
                jnp.where(half, even, pltpu.roll(odd, 4, 0)),
                jnp.where(half, pltpu.roll(even, 4, 0), odd),
            ], axis=0))
        solved = dot6(jnp.concatenate(pair, axis=1), table_ref)
        for side in range(2):
            for k in range(2):
                lr_s[side, 2 * b + k] = solved[8 * side:8 * side + 8, k * LANES:(k + 1) * LANES]
        return 0

    lax.fori_loop(0, YT // 2, solve, 0)

    def carry(side, _):
        for t, part in enumerate(y_carry([lr_s[side, t] for t in range(YT)], edge)):
            lr_s[side, t] = part
        return 0

    lax.fori_loop(0, 2, carry, 0)

    def chunk(i, _):
        come, leave = moves(i)
        come.wait()

        def row(r, _):
            x = i * FIN + r
            at = pl.ds(pl.multiple_of(x * ROW, ROW), ROW)
            low, high = (lr_s[side].reshape(ROW, LANES) for side in range(2))
            v_s[at, :] = v_s[at, :] + pow_ref[0, x] * low + pow_ref[0, X - 1 - x] * high
            return 0

        lax.fori_loop(0, FIN, row, 0, unroll=2)
        leave.start()
        return 0

    lax.fori_loop(0, X // FIN, chunk, 0)
    for i in range(X // FIN):
        moves(i)[1].wait()


def finish(powers, got, tables, v):
    vm = pl.BlockSpec(memory_space=pltpu.VMEM)
    hbm = pl.BlockSpec(memory_space=pltpu.HBM)
    return pl.pallas_call(
        final_kernel,
        in_specs=[pl.BlockSpec(memory_space=pltpu.SMEM)] + [vm] * 3 + [hbm],
        out_specs=hbm,
        out_shape=jax.ShapeDtypeStruct((ROWS, LANES), F32),
        scratch_shapes=[
            pltpu.VMEM((ROWS, LANES), F32),
            pltpu.VMEM((2, YT, Z, LANES), F32),
            pltpu.SemaphoreType.DMA((X // FIN,)),
            pltpu.SemaphoreType.DMA((X // FIN,)),
        ],
        compiler_params=vmem(50),
        cost_estimate=pl.CostEstimate(flops=10**7, bytes_accessed=10 * 2**20, transcendentals=0),
        name="finish",
    )(powers, got, *tables, v)


def shift(value, axis, forward):
    count = lax.axis_size(axis)
    pairs = [(i, i + 1) for i in range(count - 1)]
    if not forward:
        pairs = [(b, a) for a, b in pairs]
    return lax.ppermute(value, axis, pairs)


def to_tiles(block):
    return block.reshape(X, Z, YT, LANES).transpose(0, 2, 1, 3).reshape(ROWS, LANES)


def from_tiles(rows):
    return rows.reshape(X, YT, Z, LANES).transpose(0, 2, 1, 3).reshape(X, Z, Y)


def per_device(concentration, psi_level, tile_mask):
    c, level = to_tiles(concentration), to_tiles(psi_level)
    xy, gz = lax.axis_index("xy"), lax.axis_index("gz")
    n_xy, n_gz = lax.axis_size("xy"), lax.axis_size("gz")
    flags = jnp.stack([xy > 0, xy < n_xy - 1, gz > 0, gz < n_gz - 1]).astype(F32)
    mask_row = lax.dynamic_index_in_dim(tile_mask, xy * X // TILE, 0, keepdims=False)
    act = mask_row.astype(F32) * (2.0 * TIME_STEP)
    tables = tuple(jnp.asarray(t) for t in y_tables())
    steps = np.exp(-THETA * np.arange(X + 1))
    powers = jnp.asarray(np.stack([steps[1:], GAIN * steps[:-1]]).astype(np.float32))

    zlo, zhi, inner, xlo, xhi = make_faces(c, level)
    pair = (2, 2, YT, Z, LANES)
    got_xlo = shift(xhi, "xy", True).reshape(pair)
    got_xhi = shift(xlo, "xy", False).reshape(pair)
    got_zlo = shift(zhi, "gz", True)
    got_zhi = shift(zlo, "gz", False)

    def corners(z):
        return jnp.stack([got_xlo[0, 1, :, z], got_xlo[1, 1, :, z], got_xhi[0, 0, :, z], got_xhi[1, 0, :, z]])

    corner_lo = shift(corners(7), "gz", True)
    corner_hi = shift(corners(0), "gz", False)

    pot, u, mom, edgepot = solve_block(flags, act, c, level, got_xlo, got_xhi)
    df, dpot, send = add_seams(
        flags, powers, zlo, zhi, inner, got_zlo, got_zhi, got_xlo, got_xhi, corner_lo, corner_hi, edgepot, mom, act,
    )
    got = lax.all_to_all(send, "xy", split_axis=0, concat_axis=0, tiled=True)
    v = solve_lines(u, df, tables)
    got, v = lax.optimization_barrier((got, v))
    carried, pot = lax.optimization_barrier((scan_carries(got), pot))
    back = lax.all_to_all(carried, "xy", split_axis=0, concat_axis=0, tiled=True)
    potential = mend_potential(pot, dpot)
    increment = finish(powers, back, tables, v.reshape(ROWS, LANES))
    return from_tiles(potential), from_tiles(increment)


def solution(mesh):
    placed = (P("xy", "gz", None), P("xy", "gz", None), P())
    return jax.shard_map(
        per_device,
        mesh=mesh,
        in_specs=placed,
        out_specs=(P("xy", "gz", None), P("xy", "gz", None)),
        check_vma=False,
    )
```

```python
import functools
import math

import jax
import jax.numpy as jnp
import numpy as np
from jax import lax
from jax.experimental import pallas as pl
from jax.experimental.pallas import tpu as pltpu
from jax.sharding import PartitionSpec as P

TILE = 128
LEVELS = 4096
STIFF = 4096
GRADIENT_COEF = 0.5
TIME_STEP = 32.0
PSI_FLOOR = 0.25

X = 64
Z = 8
Y = 2048
YT = 16
LANES = 128
ROW = YT * Z
ROWS = X * ROW
FACE = X * YT
LINE = 2048
NB = 256
F32 = jnp.float32
BF16 = jnp.bfloat16

_half = 1.0 + 0.5 / STIFF
THETA = math.log(_half + math.sqrt(_half * _half - 1.0))
RHO = math.exp(-THETA)
GAIN = (RHO / STIFF) / (1.0 - RHO * RHO)


def rho(power):
    return math.exp(-THETA * power)


def vmem(limit_mib):
    return pltpu.CompilerParams(vmem_limit_bytes=limit_mib * 2**20)


def half_over_psi(level):
    return recip(2.0 * PSI_FLOOR + level.astype(F32) * (2.0 * (1.0 - PSI_FLOOR) / (LEVELS - 1)))


def recip(value):
    return pl.reciprocal(value, approx=True)


def lane_iota(shape):
    return lax.broadcasted_iota(jnp.int32, shape, len(shape) - 1)


def sub_iota(shape):
    return lax.broadcasted_iota(jnp.int32, shape, len(shape) - 2)


def next_y(v):
    axis = v.ndim - 1
    turned = pltpu.roll(v, LANES - 1, axis)
    if TILES_LEAD[v.shape[-2]]:
        following = jnp.concatenate([turned[1:], turned[:1]], axis=0)
    else:
        following = pltpu.roll(turned, YT - 1, axis - 1)
    return jnp.where(lane_iota(v.shape) == LANES - 1, following, turned)


def prev_y(v):
    axis = v.ndim - 1
    turned = pltpu.roll(v, 1, axis)
    if TILES_LEAD[v.shape[-2]]:
        previous = jnp.concatenate([turned[-1:], turned[:-1]], axis=0)
    else:
        previous = pltpu.roll(turned, 1, axis - 1)
    return jnp.where(lane_iota(v.shape) == 0, previous, turned)


TILES_LEAD = {Z: True, YT: False}


def next_z(v):
    return pltpu.roll(v, Z - 1, 1)


def prev_z(v):
    return pltpu.roll(v, 1, 1)


CHUNK = 8
NCHUNK = X // CHUNK
PART = CHUNK * YT


def faces_kernel(c_hbm, l_hbm, zlo_hbm, zhi_hbm, in_hbm, xlo_ref, xhi_ref, c_s, l_s, z_s, i_s, in_sem, out_sem):
    def arrivals(i):
        at = pl.ds(i * CHUNK * ROW, CHUNK * ROW)
        return (pltpu.make_async_copy(c_hbm.at[at], c_s.at[at], in_sem.at[0, i]),
                pltpu.make_async_copy(l_hbm.at[at], l_s.at[at], in_sem.at[1, i]))

    def departures(i):
        at = pl.ds(i * PART, PART)
        pairs = ((z_s.at[0, :, at], zlo_hbm.at[:, at]), (z_s.at[1, :, at], zhi_hbm.at[:, at]),
                 (i_s.at[:, at], in_hbm.at[:, at]))
        return [pltpu.make_async_copy(near, far, out_sem.at[k, i]) for k, (near, far) in enumerate(pairs)]

    for i in range(NCHUNK):
        for copy in arrivals(i):
            copy.start()

    def chunk(i, _):
        for copy in arrivals(i):
            copy.wait()
        out = pl.ds(i * PART, PART)

        def plane(ref, z):
            return ref[pl.ds(i * CHUNK * ROW + z, PART, stride=Z), :]

        for side, edge, inner in ((0, 0, 1), (1, 7, 6)):
            c_edge, c_inner = plane(c_s, edge), plane(c_s, inner)
            h_edge = half_over_psi(plane(l_s, edge))
            h_inner = half_over_psi(plane(l_s, inner))
            z_s[side, 0, out] = c_edge
            z_s[side, 1, out] = h_edge
            z_s[side, 2, out] = recip(h_edge + h_inner) * (c_inner - c_edge)
            i_s[side, out] = h_inner
        for copy in departures(i):
            copy.start()
        return 0

    lax.fori_loop(0, NCHUNK, chunk, 0)
    last = (X - 2) * ROW
    for ref, at in ((xlo_ref, 0), (xhi_ref, last)):
        ref[0] = c_s[at:at + 2 * ROW, :]
        ref[1] = l_s[at:at + 2 * ROW, :].astype(F32)
    for i in range(NCHUNK):
        for copy in departures(i):
            copy.wait()


def make_faces(c, level):
    hbm = pl.BlockSpec(memory_space=pltpu.HBM)
    vm = pl.BlockSpec(memory_space=pltpu.VMEM)
    return pl.pallas_call(
        faces_kernel,
        in_specs=[hbm, hbm],
        out_specs=[hbm, hbm, hbm, vm, vm],
        out_shape=[
            jax.ShapeDtypeStruct((3, FACE, LANES), F32),
            jax.ShapeDtypeStruct((3, FACE, LANES), F32),
            jax.ShapeDtypeStruct((2, FACE, LANES), F32),
            jax.ShapeDtypeStruct((2, 2 * ROW, LANES), F32),
            jax.ShapeDtypeStruct((2, 2 * ROW, LANES), F32),
        ],
        scratch_shapes=[
            pltpu.VMEM((ROWS, LANES), F32),
            pltpu.VMEM((ROWS, LANES), jnp.int32),
            pltpu.VMEM((2, 3, FACE, LANES), F32),
            pltpu.VMEM((2, FACE, LANES), F32),
            pltpu.SemaphoreType.DMA((2, NCHUNK)),
            pltpu.SemaphoreType.DMA((3, NCHUNK)),
        ],
        compiler_params=vmem(50),
        cost_estimate=pl.CostEstimate(flops=10**6, bytes_accessed=13 * 2**20, transcendentals=0),
        name="faces",
    )(c, level)


def y_tables():
    idx = np.arange(NB)
    table = GAIN * np.exp(-THETA * np.abs(idx[:, None] - idx[None, :]))
    parts, rest = [], table
    for _ in range(3):
        parts.append(rest.astype(jnp.bfloat16))
        rest = rest - parts[-1].astype(np.float64)
    fwd = np.exp(-THETA * (idx + 1.0))
    bwd = np.exp(-THETA * (NB - idx.astype(np.float64)))
    edge = np.zeros((8, LANES), np.float32)
    edge[0], edge[1] = fwd[:LANES], fwd[LANES:]
    edge[2], edge[3] = bwd[:LANES], bwd[LANES:]
    return np.stack(parts), edge


def split(v):
    high = v.astype(BF16)
    rest = v - high.astype(F32)
    middle = rest.astype(BF16)
    return high, middle, (rest - middle.astype(F32)).astype(BF16)


def dot6(value, table_ref):
    terms = split(value)
    rows = value.shape[0]
    total = None
    for k in (2, 1, 0):
        left = jnp.concatenate(terms[:3 - k], axis=0) if k < 2 else terms[0]
        product = jnp.dot(left, table_ref[k], preferred_element_type=F32)
        for i in reversed(range(3 - k)):
            piece = product[i * rows:(i + 1) * rows]
            total = piece if total is None else total + piece
    return total


def ends(first, last, length):
    scale = 1.0 / (1.0 - rho(2 * length))
    tail = rho(length)
    return (first + tail * last) * scale, (last + tail * first) * scale


def y_carry(tiles, edge):
    count = YT // 2
    heads = [jnp.broadcast_to(tiles[2 * b][:, 0:1], (8, LANES)) for b in range(count)]
    tails = [jnp.broadcast_to(tiles[2 * b + 1][:, LANES - 1:LANES], (8, LANES)) for b in range(count)]
    hop = rho(NB)
    right = [jnp.zeros_like(heads[0])]
    for b in range(count - 1):
        right.append(hop * right[-1] + tails[b])
    left = [jnp.zeros_like(heads[0])]
    for b in range(count - 1, 0, -1):
        left.append(hop * left[-1] + heads[b])
    left = left[::-1]
    from_low, from_high = ends(heads[0] + hop * left[0], tails[-1] + hop * right[-1], Y)
    out = []
    for b in range(count):
        carry_r = right[b] + rho(NB * b) * from_low
        carry_l = left[b] + rho(NB * (count - 1 - b)) * from_high
        for k in range(2):
            out.append(tiles[2 * b + k] + carry_r * edge[k:k + 1, :] + carry_l * edge[2 + k:3 + k, :])
    return out


MROWS = 16


def block_kernel(flag_ref, act_ref, c_hbm, l_hbm, xlo_ref, xhi_ref,
                 pot_hbm, u_hbm, mom_ref, edgepot_ref,
                 c_s, l_s, pot_s, u_s, st, in_sem, pot_sem, u_sem):
    def copies_in(i):
        at = pl.ds(i * CHUNK, CHUNK)
        return (pltpu.make_async_copy(c_hbm.at[at], c_s.at[pl.ds(i * CHUNK + 3, CHUNK)], in_sem.at[0, i]),
                pltpu.make_async_copy(l_hbm.at[at], l_s.at[pl.ds(i * CHUNK + 3, CHUNK)], in_sem.at[1, i]))

    for i in range(NCHUNK):
        for copy in copies_in(i):
            copy.start()

    tile = (Z, LANES)
    sub, lane = sub_iota(tile), lane_iota(tile)
    top, first, last = sub == Z - 1, lane == 0, lane == LANES - 1
    WZ, WY, WX, BASE, REST, POT, SWEEP, H1, H2 = range(9)

    def up_z(v):
        return pltpu.roll(v, Z - 1, 0)

    def down_z(v):
        return pltpu.roll(v, 1, 0)

    def up_y(v):
        return pltpu.roll(v, LANES - 1, 1)

    def down_y(v):
        return pltpu.roll(v, 1, 1)

    def ptile(e, t):
        return pl.ds(pl.multiple_of(e * ROW + t * Z, Z), Z)

    def advance(e, load, store):
        open_x = jnp.where(e <= 3, open_lo, jnp.where(e >= X + 3, open_hi, 1.0))
        inside = jnp.where(e >= 5, 1.0, 0.0)
        h = half_over_psi(l_s[e, 0])
        up_h, up_c = up_y(h), up_y(c_s[e, 0])
        below = below2 = jnp.zeros(tile, F32)
        held = None

        def second(t, pot1, up_pot, gx2, wz, wy, up_next, below2):
            gz = wz * (up_z(pot1) - pot1)
            gy = wy * (jnp.where(last, up_next, up_pot) - pot1)
            turned = down_y(gy)
            store(REST, t, (gz - down_z(gz)) + (gy - jnp.where(first, below2, turned)) - gx2)
            return turned

        for t in range(YT):
            c = c_s[e, t]
            if t + 1 < YT:
                h_next = half_over_psi(l_s[e, t + 1])
                up_h_next, up_c_next = up_y(h_next), up_y(c_s[e, t + 1])
            else:
                h_next, up_h_next, up_c_next = h, up_h, up_c
            h1 = load(H1, t)
            wx = recip(h1 + h) * open_x
            fx = wx * (c - c_s[e - 1, t])
            pot1 = load(BASE, t) - h1 * fx
            gx2 = load(WX, t) * (pot1 - load(POT, t))
            rhs = (act_ref[t] * inside) * (load(H2, t) * (load(REST, t) + gx2))
            swept = RHO * load(SWEEP, t) + rhs
            u_s[e, t] = swept
            pot_s[ptile(e, t), :] = pot1
            wz_old, wy_old = load(WZ, t), load(WY, t)
            wz = jnp.where(top, 0.0, recip(h + up_z(h)))
            wy = recip(h + jnp.where(last, up_h_next, up_h))
            if t == YT - 1:
                wy = jnp.where(last, 0.0, wy)
            fz = wz * (up_z(c) - c)
            fy = wy * (jnp.where(last, up_c_next, up_c) - c)
            turned = down_y(fy)
            total = (fz - down_z(fz)) + (fy - jnp.where(first, below, turned)) - fx
            below = turned
            for kind, value in ((SWEEP, swept), (POT, pot1), (BASE, c * (c * c - 1.0) - h * total),
                                (WZ, wz), (WY, wy), (WX, wx), (H1, h), (H2, h1)):
                store(kind, t, value)
            up_pot = up_y(pot1)
            if held is not None:
                below2 = second(*held, up_pot, below2)
            held = (t, pot1, up_pot, gx2, wz_old, wy_old)
            h, up_h, up_c = h_next, up_h_next, up_c_next
            yield
        second(*held, held[2], below2)
        yield

    def two_rows(e):
        between = {}

        def keep(kind, t, value):
            between[kind, t] = value

        def put(kind, t, value):
            st[kind, t] = value

        ahead = advance(e, lambda kind, t: st[kind, t], keep)
        behind = advance(e + 1, lambda kind, t: between.pop((kind, t)), put)
        next(ahead)
        for _ in range(YT):
            next(ahead)
            next(behind)
        next(behind)

    open_lo, open_hi = flag_ref[0], flag_ref[1]
    st[...] = jnp.zeros_like(st)
    st[H1:] = jnp.ones((2, YT, Z, LANES), F32)
    c_s[0] = jnp.zeros((YT, Z, LANES), F32)
    for at, ref in ((1, xlo_ref), (X + 3, xhi_ref)):
        c_s[at:at + 2] = ref[0]
        l_s[at:at + 2] = ref[1].astype(jnp.int32)

    def pot_copy(i):
        src = pl.ds((i * CHUNK + 4) * ROW, CHUNK * ROW)
        return pltpu.make_async_copy(pot_s.at[src], pot_hbm.at[pl.ds(i * CHUNK * ROW, CHUNK * ROW)], pot_sem.at[i])

    pairs = CHUNK // 2

    def rows(j, _):
        turn = lax.rem(j, pairs) == 1

        @pl.when(jnp.logical_and(turn, j < X // 2))
        def _():
            for copy in copies_in((j - 1) // pairs):
                copy.wait()

        two_rows(2 * j + 1)

        @pl.when(jnp.logical_and(turn, j > pairs))
        def _():
            pot_copy((j - 1) // pairs - 1).start()
        return 0

    lax.fori_loop(0, X // 2 + 2, rows, 0)

    def u_copy(i):
        src = pl.ds(i * CHUNK + 5, CHUNK)
        return pltpu.make_async_copy(u_s.at[src], u_hbm.at[pl.ds(i * CHUNK, CHUNK)], u_sem.at[i])

    def back(k, carry):
        x = X - 1 - k
        mine, after = carry
        before = u_s[x + 4]
        u_s[x + 5] = GAIN * (mine + after)

        @pl.when(lax.rem(x, CHUNK) == 0)
        def _():
            u_copy(x // CHUNK).start()
        return before, RHO * (after + (mine - RHO * before))

    lax.fori_loop(0, X, back, (u_s[X + 4], jnp.zeros((YT, Z, LANES), F32)))
    mom_ref[0] = u_s[X + 4]
    mom_ref[1] = u_s[5]
    for side, z in ((0, 0), (1, 7)):
        edgepot_ref[side] = pot_s[pl.ds(4 * ROW + z, FACE, stride=Z), :]

    for i in range(NCHUNK):
        pot_copy(i).wait()
        u_copy(i).wait()


def solve_block(flags, act, c, level, xlo, xhi):
    any_spec = pl.BlockSpec(memory_space=pltpu.HBM)
    vm = pl.BlockSpec(memory_space=pltpu.VMEM)
    sm = pl.BlockSpec(memory_space=pltpu.SMEM)
    block = (X, YT, Z, LANES)
    return pl.pallas_call(
        block_kernel,
        in_specs=[sm, sm, any_spec, any_spec, vm, vm],
        out_specs=[any_spec, any_spec, vm, vm],
        out_shape=[
            jax.ShapeDtypeStruct((ROWS, LANES), F32),
            jax.ShapeDtypeStruct(block, F32),
            jax.ShapeDtypeStruct((2, YT, Z, LANES), F32),
            jax.ShapeDtypeStruct((2, FACE, LANES), F32),
        ],
        scratch_shapes=[
            pltpu.VMEM((X + 5, YT, Z, LANES), F32),
            pltpu.VMEM((X + 5, YT, Z, LANES), jnp.int32),
            pltpu.VMEM(((X + 5) * ROW, LANES), F32),
            pltpu.VMEM((X + 5, YT, Z, LANES), F32),
            pltpu.VMEM((9, YT, Z, LANES), F32),
            pltpu.SemaphoreType.DMA((2, NCHUNK)),
            pltpu.SemaphoreType.DMA((NCHUNK,)),
            pltpu.SemaphoreType.DMA((NCHUNK,)),
        ],
        compiler_params=vmem(50),
        cost_estimate=pl.CostEstimate(flops=4 * 10**9, bytes_accessed=60 * 2**20, transcendentals=0),
        name="block",
    )(flags, act, c.reshape(block), level.reshape(block), xlo, xhi)


EXT = X + 2
GROUP = 8


def seam_kernel(flag_ref, pow_ref, own_lo, own_hi, inner_hbm, got_lo, got_hi, xlo_ref, xhi_ref,
                corner_lo_ref, corner_hi_ref, edgepot_hbm, mom_ref, act_ref,
                df_hbm, dpot_hbm, send_ref, ext_s, in_s, df_s, dpot_s, fl_s, acc_s, in_sem, out_sem):
    open_x = (flag_ref[0], flag_ref[1])
    tile_row = lax.broadcasted_iota(jnp.int32, (YT, LANES), 0)
    act = jnp.zeros((YT, LANES), F32)
    for t in range(YT):
        act = jnp.where(tile_row == t, act_ref[t], act)
    shape = (GROUP, YT, LANES)
    open_y = jnp.logical_or(
        lax.broadcasted_iota(jnp.int32, shape, 2) < LANES - 1,
        lax.broadcasted_iota(jnp.int32, shape, 1) < YT - 1,
    )
    row = lax.broadcasted_iota(jnp.int32, shape, 0)
    acc_s[...] = jnp.zeros_like(acc_s)
    main = pl.ds(1, X)

    def arrivals(side):
        own, got = ((own_lo, got_lo), (own_hi, got_hi))[side]
        pairs = [(own.at[0], ext_s.at[side, 0, main]), (own.at[1], ext_s.at[side, 1, main]),
                 (got.at[0], ext_s.at[side, 2, main]), (got.at[1], ext_s.at[side, 3, main]),
                 (got.at[2], in_s.at[side, 0]), (inner_hbm.at[side], in_s.at[side, 1]),
                 (edgepot_hbm.at[side], in_s.at[side, 2])]
        return [pltpu.make_async_copy(far, near, in_sem.at[side, k]) for k, (far, near) in enumerate(pairs)]

    def departures(side):
        at = pl.ds(2 * side, 2)
        return [pltpu.make_async_copy(df_s.at[at], df_hbm.at[at], out_sem.at[side, 0]),
                pltpu.make_async_copy(dpot_s.at[side], dpot_hbm.at[side], out_sem.at[side, 1])]

    for side in range(2):
        for copy in arrivals(side):
            copy.start()

    for side, (corner, z) in enumerate(((corner_lo_ref, 0), (corner_hi_ref, 7))):
        for spot, ref, r, k in ((0, xlo_ref, 1, 0), (EXT - 1, xhi_ref, 0, 1)):
            ext_s[side, 0, spot] = ref[0, r, :, z, :]
            ext_s[side, 1, spot] = half_over_psi(ref[1, r, :, z, :])
            ext_s[side, 2, spot] = corner[2 * k]
            ext_s[side, 3, spot] = half_over_psi(corner[2 * k + 1])

    def one_side(side, _):
        for k in range(2):
            @pl.when(side == k)
            def _():
                for copy in arrivals(k)[:4]:
                    copy.wait()
        open_z = flag_ref[2 + side]
        bias = 1.0 - open_z
        c0_s, h0_s, cm_s, hm_s, dp_s = (ext_s.at[side, k] for k in range(5))
        got2_s, inner_s, pot_s = (in_s.at[side, k] for k in range(3))

        def first(i, _):
            at = pl.ds(i * 6, 6)
            h0 = h0_s[at]
            flux = recip(h0 + hm_s[at]) * open_z * (cm_s[at] - c0_s[at])
            fl_s[at] = flux
            dp_s[at] = -h0 * flux
            return 0

        lax.fori_loop(0, EXT // 6, first, 0)
        for k in range(2):
            @pl.when(side == k)
            def _():
                for copy in arrivals(k)[4:]:
                    copy.wait()

        def second(i, _):
            at = pl.ds(i * GROUP, GROUP)
            ext = pl.ds(i * GROUP + 1, GROUP)
            after = pl.ds(i * GROUP + 2, GROUP)
            lo_gate = jnp.where(row == 0, jnp.where(i == 0, open_x[0], 1.0), 1.0)
            hi_gate = jnp.where(row == GROUP - 1, jnp.where(i == X // GROUP - 1, open_x[1], 1.0), 1.0)

            def plane(h_ref, v_ref, extra):
                h, v = h_ref[ext] + extra, v_ref[ext]
                wy = jnp.where(open_y, recip(h + next_y(h)), 0.0)
                fy = wy * (next_y(v) - v)
                total = recip(h + h_ref[at]) * lo_gate * (v_ref[at] - v)
                total = total + recip(h + h_ref[after]) * hi_gate * (v_ref[after] - v)
                return h, v, total + (fy - prev_y(fy))

            hm, cm, across_m = plane(hm_s, cm_s, bias)
            h0, dp, across_0 = plane(h0_s, dp_s, 0.0)
            flux = fl_s[ext]
            potm = cm * (cm * cm - 1.0) - hm * (across_m + got2_s[at] - flux)
            pot0 = pot_s[at] + dp
            h1 = inner_s[at]
            toward = recip(h0 + h1) * dp
            join = recip(h0 + hm) * open_z * (potm - pot0)
            df0 = act * (h0 * (across_0 - toward + join))
            df1 = act * (h1 * toward)
            outer, inner = 3 * side, 1 + side
            df_s[outer, at] = df0
            df_s[inner, at] = df1
            dpot_s[side, at] = dp
            for spot, value in ((outer, df0), (inner, df1)):
                last, start = acc_s[spot], acc_s[4 + spot]
                for r in range(GROUP):
                    x = i * GROUP + r
                    last = last + pow_ref[1, X - 1 - x] * value[r]
                    start = start + pow_ref[1, x] * value[r]
                acc_s[spot] = last
                acc_s[4 + spot] = start
            return 0

        lax.fori_loop(0, X // GROUP, second, 0)
        for copy in departures(side):
            copy.start()
        return 0

    lax.fori_loop(0, 2, one_side, 0)

    sub = sub_iota((Z, LANES))
    half = sub < 4
    for t in range(YT):
        totals = []
        for which in range(2):
            total = mom_ref[which, t]
            for k, z in enumerate((0, 1, 6, 7)):
                line = jnp.broadcast_to(acc_s[4 * which + k, t:t + 1, :], (Z, LANES))
                total = total + jnp.where(sub == z, line, 0.0)
            totals.append(total)
        last, start = totals
        send_ref[2 * t] = jnp.where(half, last, pltpu.roll(start, 4, 0))
        send_ref[2 * t + 1] = jnp.where(half, pltpu.roll(last, 4, 0), start)
    for side in range(2):
        for copy in departures(side):
            copy.wait()


def add_seams(flags, powers, own_lo, own_hi, inner, got_lo, got_hi, xlo, xhi, corner_lo, corner_hi, edgepot, mom, act):
    vm = pl.BlockSpec(memory_space=pltpu.VMEM)
    sm = pl.BlockSpec(memory_space=pltpu.SMEM)
    hbm = pl.BlockSpec(memory_space=pltpu.HBM)
    lines = [a.reshape(a.shape[0], X, YT, LANES) for a in (own_lo, own_hi, inner, got_lo, got_hi)]
    return pl.pallas_call(
        seam_kernel,
        in_specs=[sm, sm] + [hbm] * 5 + [vm] * 4 + [hbm, vm, sm],
        out_specs=[hbm, hbm, vm],
        out_shape=[
            jax.ShapeDtypeStruct((4, X, YT, LANES), F32),
            jax.ShapeDtypeStruct((2, X, YT, LANES), F32),
            jax.ShapeDtypeStruct((32, Z, LANES), F32),
        ],
        scratch_shapes=[
            pltpu.VMEM((2, 5, EXT, YT, LANES), F32),
            pltpu.VMEM((2, 3, X, YT, LANES), F32),
            pltpu.VMEM((4, X, YT, LANES), F32),
            pltpu.VMEM((2, X, YT, LANES), F32),
            pltpu.VMEM((EXT, YT, LANES), F32),
            pltpu.VMEM((8, YT, LANES), F32),
            pltpu.SemaphoreType.DMA((2, 7)),
            pltpu.SemaphoreType.DMA((2, 2)),
        ],
        compiler_params=vmem(50),
        cost_estimate=pl.CostEstimate(flops=10**7, bytes_accessed=12 * 2**20, transcendentals=0),
        name="seams",
    )(flags, powers, *lines, xlo, xhi, corner_lo, corner_hi, edgepot.reshape(2, X, YT, LANES), mom, act)


def lines_kernel(u_hbm, df_hbm, table_ref, edge_ref, out_hbm, u_s, df_s, p_s, w_s, v_s, df_sem, in_sem, out_sem):
    groups = X // MROWS
    grow = MROWS * ROW

    def moves(i):
        at = pl.ds(i * MROWS, MROWS)
        return (pltpu.make_async_copy(u_hbm.at[pl.ds(i * grow, grow)], u_s.at[pl.ds(i * grow, grow)], in_sem.at[i]),
                pltpu.make_async_copy(v_s.at[at], out_hbm.at[at], out_sem.at[i]))

    bring = pltpu.make_async_copy(df_hbm, df_s, df_sem)
    bring.start()
    for i in range(groups):
        moves(i)[0].start()
    bring.wait()
    shape = (4, YT, LANES)

    def forth(x, carry):
        carry = RHO * carry + df_s[:, x]
        p_s[:, x] = carry
        return carry

    lax.fori_loop(0, X, forth, jnp.zeros(shape, F32), unroll=4)

    def back(k, carry):
        x = X - 1 - k
        f = df_s[:, x]
        df_s[:, x] = GAIN * (p_s[:, x] + carry)
        return RHO * (carry + f)

    lax.fori_loop(0, X, back, jnp.zeros(shape, F32), unroll=4)
    edge = edge_ref[...]

    def group(i, _):
        come, leave = moves(i)
        come.wait()
        for n, z in enumerate((0, 1, 6, 7)):
            at = pl.ds(i * grow + z, MROWS * YT, stride=Z)
            added = df_s[n, pl.ds(i * MROWS, MROWS)].reshape(MROWS * YT, LANES)
            u_s[at, :] = u_s[at, :] + added
        for b in range(YT // 2):
            pair = [
                jnp.concatenate([
                    u_s[pl.ds(pl.multiple_of(i * grow + x * ROW + (2 * b + k) * Z, Z), Z), :] for x in range(MROWS)
                ], axis=0)
                for k in range(2)
            ]
            solved = dot6(jnp.concatenate(pair, axis=1), table_ref)
            for k in range(2):
                w_s[:, 2 * b + k] = solved[:, k * LANES:(k + 1) * LANES].reshape(MROWS, Z, LANES)

        def body(x, _):
            for t, part in enumerate(y_carry([w_s[x, t] for t in range(YT)], edge)):
                v_s[i * MROWS + x, t] = part
            return 0

        lax.fori_loop(0, MROWS, body, 0, unroll=UNROLL)
        leave.start()
        return 0

    lax.fori_loop(0, groups, group, 0)
    for i in range(groups):
        moves(i)[1].wait()


UNROLL = 16


def solve_lines(u, df, tables):
    vm = pl.BlockSpec(memory_space=pltpu.VMEM)
    hbm = pl.BlockSpec(memory_space=pltpu.HBM)
    block = (X, YT, Z, LANES)
    return pl.pallas_call(
        lines_kernel,
        in_specs=[hbm, hbm] + [vm] * 2,
        out_specs=hbm,
        out_shape=jax.ShapeDtypeStruct(block, F32),
        scratch_shapes=[
            pltpu.VMEM((ROWS, LANES), F32),
            pltpu.VMEM((4, X, YT, LANES), F32),
            pltpu.VMEM((4, X, YT, LANES), F32),
            pltpu.VMEM((MROWS, YT, Z, LANES), F32),
            pltpu.VMEM(block, F32),
            pltpu.SemaphoreType.DMA,
            pltpu.SemaphoreType.DMA((X // MROWS,)),
            pltpu.SemaphoreType.DMA((X // MROWS,)),
        ],
        compiler_params=vmem(50),
        cost_estimate=pl.CostEstimate(flops=2 * 10**9, bytes_accessed=10 * 2**20, transcendentals=0),
        name="lines",
    )(u.reshape(ROWS, LANES), df, *tables)


def mend_kernel(pot_hbm, dpot_hbm, out_hbm, pot_s, dpot_s, in_sem, out_sem):
    def moves(i):
        at, part = pl.ds(i * CHUNK * ROW, CHUNK * ROW), pl.ds(i * PART, PART)
        return (pltpu.make_async_copy(pot_hbm.at[at], pot_s.at[at], in_sem.at[0, i]),
                pltpu.make_async_copy(dpot_hbm.at[:, part], dpot_s.at[:, part], in_sem.at[1, i]),
                pltpu.make_async_copy(pot_s.at[at], out_hbm.at[at], out_sem.at[i]))

    for i in range(NCHUNK):
        moves(i)[0].start()
        moves(i)[1].start()

    def chunk(i, _):
        pot_in, dpot_in, leave = moves(i)
        pot_in.wait()
        dpot_in.wait()
        for side, z in ((0, 0), (1, 7)):
            at = pl.ds(i * CHUNK * ROW + z, PART, stride=Z)
            pot_s[at, :] = pot_s[at, :] + dpot_s[side, pl.ds(i * PART, PART), :]
        leave.start()
        return 0

    lax.fori_loop(0, NCHUNK, chunk, 0)
    for i in range(NCHUNK):
        moves(i)[2].wait()


def mend_potential(pot, dpot):
    hbm = pl.BlockSpec(memory_space=pltpu.HBM)
    return pl.pallas_call(
        mend_kernel,
        in_specs=[hbm, hbm],
        out_specs=hbm,
        out_shape=jax.ShapeDtypeStruct((ROWS, LANES), F32),
        scratch_shapes=[
            pltpu.VMEM((ROWS, LANES), F32),
            pltpu.VMEM((2, FACE, LANES), F32),
            pltpu.SemaphoreType.DMA((2, NCHUNK)),
            pltpu.SemaphoreType.DMA((NCHUNK,)),
        ],
        compiler_params=vmem(50),
        cost_estimate=pl.CostEstimate(flops=10**7, bytes_accessed=10 * 2**20, transcendentals=0),
        name="mend",
    )(pot, dpot.reshape(2, FACE, LANES))


def carries_kernel(count, in_ref, out_ref):
    got = [in_ref[d] for d in range(count)]
    half = sub_iota((8, TILE)) < 4
    hop = rho(X)
    right = [jnp.zeros((8, TILE), F32)]
    for d in range(count - 1):
        right.append(hop * right[-1] + got[d])
    starts = [pltpu.roll(g, 4, 0) for g in got]
    left = [jnp.zeros((8, TILE), F32)]
    for d in range(count - 1, 0, -1):
        left.append(hop * left[-1] + starts[d])
    left = left[::-1]
    from_low, from_high = ends(starts[0] + hop * left[0], got[-1] + hop * right[-1], X * count)
    for d in range(count):
        carry_r = right[d] + rho(X * d) * from_low
        carry_l = left[d] + rho(X * (count - 1 - d)) * from_high
        out_ref[d] = jnp.where(half, carry_r, pltpu.roll(carry_l, 4, 0))


def scan_carries(got):
    vm = pl.BlockSpec(memory_space=pltpu.VMEM)
    return pl.pallas_call(
        functools.partial(carries_kernel, got.shape[0]),
        in_specs=[vm],
        out_specs=vm,
        out_shape=jax.ShapeDtypeStruct(got.shape, F32),
        cost_estimate=pl.CostEstimate(flops=10**6, bytes_accessed=2**18, transcendentals=0),
        name="carries",
    )(got)


FIN = 8


def final_kernel(pow_ref, got_ref, table_ref, edge_ref, v_hbm, out_hbm, v_s, lr_s, in_sem, out_sem):
    def moves(i):
        at = pl.ds(i * FIN * ROW, FIN * ROW)
        return (pltpu.make_async_copy(v_hbm.at[at], v_s.at[at], in_sem.at[i]),
                pltpu.make_async_copy(v_s.at[at], out_hbm.at[at], out_sem.at[i]))

    for i in range(X // FIN):
        moves(i)[0].start()
    half = sub_iota((Z, LANES)) < 4
    edge = edge_ref[...]

    def solve(b, _):
        pair = []
        for k in range(2):
            even, odd = got_ref[4 * b + 2 * k], got_ref[4 * b + 2 * k + 1]
            pair.append(jnp.concatenate([
                jnp.where(half, even, pltpu.roll(odd, 4, 0)),
                jnp.where(half, pltpu.roll(even, 4, 0), odd),
            ], axis=0))
        solved = dot6(jnp.concatenate(pair, axis=1), table_ref)
        for side in range(2):
            for k in range(2):
                lr_s[side, 2 * b + k] = solved[8 * side:8 * side + 8, k * LANES:(k + 1) * LANES]
        return 0

    lax.fori_loop(0, YT // 2, solve, 0)

    def carry(side, _):
        for t, part in enumerate(y_carry([lr_s[side, t] for t in range(YT)], edge)):
            lr_s[side, t] = part
        return 0

    lax.fori_loop(0, 2, carry, 0)

    def chunk(i, _):
        come, leave = moves(i)
        come.wait()

        def row(r, _):
            x = i * FIN + r
            at = pl.ds(pl.multiple_of(x * ROW, ROW), ROW)
            low, high = (lr_s[side].reshape(ROW, LANES) for side in range(2))
            v_s[at, :] = v_s[at, :] + pow_ref[0, x] * low + pow_ref[0, X - 1 - x] * high
            return 0

        lax.fori_loop(0, FIN, row, 0, unroll=2)
        leave.start()
        return 0

    lax.fori_loop(0, X // FIN, chunk, 0)
    for i in range(X // FIN):
        moves(i)[1].wait()


def finish(powers, got, tables, v):
    vm = pl.BlockSpec(memory_space=pltpu.VMEM)
    hbm = pl.BlockSpec(memory_space=pltpu.HBM)
    return pl.pallas_call(
        final_kernel,
        in_specs=[pl.BlockSpec(memory_space=pltpu.SMEM)] + [vm] * 3 + [hbm],
        out_specs=hbm,
        out_shape=jax.ShapeDtypeStruct((ROWS, LANES), F32),
        scratch_shapes=[
            pltpu.VMEM((ROWS, LANES), F32),
            pltpu.VMEM((2, YT, Z, LANES), F32),
            pltpu.SemaphoreType.DMA((X // FIN,)),
            pltpu.SemaphoreType.DMA((X // FIN,)),
        ],
        compiler_params=vmem(50),
        cost_estimate=pl.CostEstimate(flops=10**7, bytes_accessed=10 * 2**20, transcendentals=0),
        name="finish",
    )(powers, got, *tables, v)


def shift(value, axis, forward):
    count = lax.axis_size(axis)
    pairs = [(i, i + 1) for i in range(count - 1)]
    if not forward:
        pairs = [(b, a) for a, b in pairs]
    return lax.ppermute(value, axis, pairs)


def to_tiles(block):
    return block.reshape(X, Z, YT, LANES).transpose(0, 2, 1, 3).reshape(ROWS, LANES)


def from_tiles(rows):
    return rows.reshape(X, YT, Z, LANES).transpose(0, 2, 1, 3).reshape(X, Z, Y)


def per_device(concentration, psi_level, tile_mask):
    c, level = to_tiles(concentration), to_tiles(psi_level)
    xy, gz = lax.axis_index("xy"), lax.axis_index("gz")
    n_xy, n_gz = lax.axis_size("xy"), lax.axis_size("gz")
    flags = jnp.stack([xy > 0, xy < n_xy - 1, gz > 0, gz < n_gz - 1]).astype(F32)
    mask_row = lax.dynamic_index_in_dim(tile_mask, xy * X // TILE, 0, keepdims=False)
    act = mask_row.astype(F32) * (2.0 * TIME_STEP)
    tables = tuple(jnp.asarray(t) for t in y_tables())
    steps = np.exp(-THETA * np.arange(X + 1))
    powers = jnp.asarray(np.stack([steps[1:], GAIN * steps[:-1]]).astype(np.float32))

    zlo, zhi, inner, xlo, xhi = make_faces(c, level)
    pair = (2, 2, YT, Z, LANES)
    got_xlo = shift(xhi, "xy", True).reshape(pair)
    got_xhi = shift(xlo, "xy", False).reshape(pair)
    got_zlo = shift(zhi, "gz", True)
    got_zhi = shift(zlo, "gz", False)

    def corners(z):
        return jnp.stack([got_xlo[0, 1, :, z], got_xlo[1, 1, :, z], got_xhi[0, 0, :, z], got_xhi[1, 0, :, z]])

    corner_lo = shift(corners(7), "gz", True)
    corner_hi = shift(corners(0), "gz", False)

    pot, u, mom, edgepot = solve_block(flags, act, c, level, got_xlo, got_xhi)
    df, dpot, send = add_seams(
        flags, powers, zlo, zhi, inner, got_zlo, got_zhi, got_xlo, got_xhi, corner_lo, corner_hi, edgepot, mom, act,
    )
    got = lax.all_to_all(send, "xy", split_axis=0, concat_axis=0, tiled=True)
    potential = mend_potential(pot, dpot)
    got, potential = lax.optimization_barrier((got, potential))
    carried, u = lax.optimization_barrier((scan_carries(got), u))
    back = lax.all_to_all(carried, "xy", split_axis=0, concat_axis=0, tiled=True)
    v = solve_lines(u, df, tables)
    increment = finish(powers, back, tables, v.reshape(ROWS, LANES))
    return from_tiles(potential), from_tiles(increment)


def solution(mesh):
    placed = (P("xy", "gz", None), P("xy", "gz", None), P())
    return jax.shard_map(
        per_device,
        mesh=mesh,
        in_specs=placed,
        out_specs=(P("xy", "gz", None), P("xy", "gz", None)),
        check_vma=False,
    )
```
